32 devices in a mesh: ctx: 8 (over y, x, core), tp: 4 (over z).
Axes of the slice: x: 2, y: 2, z: 4, core: 2. Of those that a mesh axis runs over, the one named last changes fastest.
Arguments:
- gate_input: bfloat16 [2048, 8192], P('ctx', 'tp'), may hold values from -6 to 6
- value_input: bfloat16 [2048, 8192], P('ctx', 'tp'), may hold values from -6 to 6
- filter_taps: float32 [2048, 8192], P('ctx', 'tp'), may hold values from -1 to 1
- skip_gain: float32 [8192], P('tp'), may hold values from 0.3 to 3
- queries: bfloat16 [2048, 8192], P('ctx', 'tp'), may hold values from -8 to 8
- keys: bfloat16 [2048, 8192], P('ctx', 'tp'), may hold values from -8 to 8
Outputs:
- mixed: bfloat16 [2048, 8192], P('ctx', 'tp')
- attended: bfloat16 [2048, 8192], P('ctx', 'tp')
The draws below stay inside these ranges and needn't reach their ends.
All inputs are finite; a program needn't handle non-finite values.
Results may differ from the reference program's by a relative error of at most 0.012.
Values may be sent and summed in bfloat16 or wider, within the bound.
A program may use at most 128 MiB of HBM per device.

```python
import math
import jax
import jax.numpy as jnp
from jax import lax

MODEL_WIDTH = 8192
HEADS = 64
HEAD_DIM = 128
SEQUENCE_TOTAL = 2048


def draw_queries(key, part):
    key = jax.random.fold_in(key, 5)
    values = jnp.clip(jax.random.normal(key, (SEQUENCE_TOTAL, MODEL_WIDTH), dtype=jnp.float32), -6.0, 6.0)
    return values.astype(jnp.bfloat16)


def draw_keys(key, part):
    key = jax.random.fold_in(key, 6)
    values = jnp.clip(jax.random.normal(key, (SEQUENCE_TOTAL, MODEL_WIDTH), dtype=jnp.float32), -6.0, 6.0)
    return values.astype(jnp.bfloat16)


def draw_filter_taps(key, part):
    key = jax.random.fold_in(key, 7)
    decay_key, spike_key, jitter_key, polarity_key = jax.random.split(key, 4)
    lowest = math.log(16.0)
    decay_time = jnp.exp(jax.random.uniform(decay_key, (MODEL_WIDTH,), dtype=jnp.float32, minval=lowest, maxval=math.log(4.0 * SEQUENCE_TOTAL)))
    peak_height = jnp.sqrt(2.0 / jnp.minimum(decay_time, 2.0 * SEQUENCE_TOTAL))
    delay_offsets = jnp.arange(SEQUENCE_TOTAL, dtype=jnp.int32)
    spike_events = jax.random.randint(spike_key, (3, MODEL_WIDTH), 1, SEQUENCE_TOTAL)
    tally_result = jnp.sum((delay_offsets[None, :, None] >= spike_events[:, None, :]).astype(jnp.float32), axis=0)
    spike_multiplier = jnp.power(0.6, tally_result)
    jitter_noise = jax.random.uniform(jitter_key, (SEQUENCE_TOTAL, MODEL_WIDTH), dtype=jnp.float32, minval=0.5, maxval=1.5)
    jitter_noise = jitter_noise * jnp.where(jax.random.bernoulli(polarity_key, 0.5, (SEQUENCE_TOTAL, MODEL_WIDTH)), 1.0, -1.0)
    decay_curve = jnp.exp(-delay_offsets.astype(jnp.float32)[:, None] / decay_time[None, :])
    return peak_height[None, :] * decay_curve * spike_multiplier * jitter_noise


def levels(stream_key, extent, shards, smallest, top_value):
    def one(dim, shards_of):
        draws = jax.random.uniform(jax.random.fold_in(jax.random.fold_in(stream_key, 6), dim), (shards_of,), jnp.float32, smallest / len(shards), top_value / len(shards))
        return jnp.repeat(jnp.exp(draws), extent[dim] // shards_of).reshape((-1,) + (1,) * (len(extent) - dim - 1))

    loudness = one(*shards[0])
    for cut in shards[1:]:
        loudness = loudness * one(*cut)
    return loudness


def scatter_about(stream_key, shape, scale, most, shards=(), held_as=jnp.bfloat16):
    result = scale * jax.random.normal(stream_key, shape, jnp.float32)
    if shards:
        result = result * levels(stream_key, shape, shards, -0.22, 0.18)
    return jnp.clip(result, -most, most).astype(held_as)


def setup_inputs(seed: int = 0) -> dict:
    splits = jax.random.split(jax.random.key(seed), 7)
    return {
        "gate_input": scatter_about(splits[0], (SEQUENCE_TOTAL, MODEL_WIDTH), 1.0, 6.0, ((0, 8), (1, 4))),
        "value_input": scatter_about(splits[1], (SEQUENCE_TOTAL, MODEL_WIDTH), 1.0, 6.0, ((0, 8), (1, 4))),
        "filter_taps": draw_filter_taps(jax.random.fold_in(splits[6], 71), 0),
        "skip_gain": jnp.clip(jnp.exp(math.log(3.0) - 2.3025851 * jax.random.uniform(splits[3], (MODEL_WIDTH,), jnp.float32) ** levels(splits[3], (MODEL_WIDTH,), ((0, 4),), -0.2, 0.2)), 0.3, 3.0),
        "queries": draw_queries(jax.random.fold_in(splits[6], 71), 0),
        "keys": draw_keys(jax.random.fold_in(splits[6], 71), 0),
    }


def causal_filter(operands):
    signal, filter_rows = operands
    length = signal.shape[0]
    spectrum = jnp.fft.rfft(signal, n=2 * length, axis=0) * jnp.fft.rfft(filter_rows, n=2 * length, axis=0)
    return jnp.fft.irfft(spectrum, n=2 * length, axis=0)[:length]

def by_heads(matrix):
    return matrix.reshape(SEQUENCE_TOTAL, HEADS, HEAD_DIM).transpose(1, 0, 2)

def from_heads(stacked):
    return stacked.transpose(1, 0, 2).reshape(SEQUENCE_TOTAL, MODEL_WIDTH)

def one_head(triple):
    query_rows, key_rows, value_rows = triple
    scores = jnp.dot(query_rows, key_rows.T, preferred_element_type=jnp.float32) / math.sqrt(HEAD_DIM)
    position = jnp.arange(SEQUENCE_TOTAL, dtype=jnp.int32)
    allowed = position[None, :] <= position[:, None]
    masked = jnp.where(allowed, scores, -jnp.inf)
    highest = lax.optimization_barrier(jnp.max(masked, axis=1, keepdims=True))
    weights = jnp.where(allowed, jnp.exp(masked - highest), 0.0)
    total_weight = lax.optimization_barrier(jnp.sum(weights, axis=1, keepdims=True))
    numerator = jnp.dot(weights.astype(jnp.bfloat16), value_rows, preferred_element_type=jnp.float32)
    return numerator / total_weight

def reference(gate_input, value_input, filter_taps, skip_gain, queries, keys):
    signal = value_input.astype(jnp.float32)
    convolved = from_heads(lax.map(causal_filter, (by_heads(signal), by_heads(filter_taps))))
    mixed = (gate_input.astype(jnp.float32) * (convolved + skip_gain[None, :] * signal)).astype(jnp.bfloat16)
    attended = from_heads(lax.map(one_head, (by_heads(queries), by_heads(keys), by_heads(mixed))))
    return (mixed, attended.astype(jnp.bfloat16))
```

```python
import functools
import math

import jax
import jax.numpy as jnp
import numpy as np
from jax import lax
from jax.experimental import pallas as pl
from jax.experimental.pallas import tpu as pltpu
from jax.sharding import PartitionSpec as P

HEAD_DIM = 128


PRECISE = lax.Precision.HIGHEST
TWO_PI = 2.0 * math.pi


def as_sent(value):

    def short(part):
        return part.astype(jnp.bfloat16) if part.dtype == jnp.float32 else part

    return jax.tree.map(short, value)


def unit_roots(first_index, second_index, period, orient):
    product = first_index[:, None] * second_index[None, :] % period
    angles = TWO_PI / period * product.astype(jnp.float32)
    return (jnp.cos(angles), orient * jnp.sin(angles))


def first_section(signal, shards):
    cosine, sine_part = unit_roots(
        jnp.arange(2 * shards, dtype=jnp.int32),
        jnp.arange(shards, dtype=jnp.int32),
        2 * shards,
        -1.0,
    )
    real_part = jnp.einsum("kn,nmc->kmc", cosine, signal, precision=PRECISE)
    imag_part = jnp.einsum("kn,nmc->kmc", sine_part, signal, precision=PRECISE)
    return (real_part, imag_part)


def twist(real_part, imag_part, outer_index, inner_index, padded, orient):
    cosine, sine_part = unit_roots(outer_index, inner_index, padded, orient)
    cosine = cosine[:, :, None]
    sine_part = sine_part[:, :, None]
    return (real_part * cosine - imag_part * sine_part, real_part * sine_part + imag_part * cosine)


def contract(matrix, operand):
    return jnp.einsum("qn,knc->kqc", matrix, operand, precision=PRECISE)


def second_section(real_part, imag_part, orient):
    length = real_part.shape[1]
    indices = jnp.arange(length, dtype=jnp.int32)
    cosine, sine_part = unit_roots(indices, indices, length, orient)
    new_real = contract(cosine, real_part) - contract(sine_part, imag_part)
    new_imag = contract(sine_part, real_part) + contract(cosine, imag_part)
    return (new_real, new_imag)


def last_section(real_part, imag_part, shards, padded):
    cosine, sine_part = unit_roots(
        jnp.arange(shards, dtype=jnp.int32),
        jnp.arange(2 * shards, dtype=jnp.int32),
        2 * shards,
        1.0,
    )
    summed = jnp.einsum("nk,kmc->nmc", cosine, real_part, precision=PRECISE) - jnp.einsum(
        "nk,kmc->nmc", sine_part, imag_part, precision=PRECISE
    )
    return summed * (1.0 / padded)


def spectral_product(signal_spectrum, filter_spectrum):
    signal_real, signal_imag = signal_spectrum
    filter_real, filter_imag = filter_spectrum
    return (
        signal_real * filter_real - signal_imag * filter_imag,
        signal_real * filter_imag + signal_imag * filter_real,
    )


def by_sequence(gate_input, value_input, filter_taps, skip_gain, queries, keys):
    shards = lax.axis_size("ctx")
    my_index = lax.axis_index("ctx")
    tok_rows, channels = value_input.shape
    padded = 2 * shards * tok_rows
    signal = value_input.astype(jnp.float32)
    wide_index = jnp.arange(2 * shards, dtype=jnp.int32)
    slab_rows = tok_rows // shards
    moved_signal, moved_taps = (
        lax.all_to_all(
            signal.reshape(1, tok_rows, channels).astype(jnp.bfloat16),
            "ctx",
            split_axis=1,
            concat_axis=0,
            tiled=True,
        ).astype(jnp.float32),
        lax.all_to_all(
            filter_taps.reshape(1, tok_rows, channels).astype(jnp.bfloat16),
            "ctx",
            split_axis=1,
            concat_axis=0,
            tiled=True,
        ).astype(jnp.float32),
    )
    inner_index = my_index * slab_rows + jnp.arange(slab_rows, dtype=jnp.int32)

    def spread_front(block):
        real_part, imag_part = first_section(block, shards)
        real_part, imag_part = twist(real_part, imag_part, wide_index, inner_index, padded, -1.0)
        return jnp.stack([real_part, imag_part])

    turned_signal, turned_taps = (
        lax.all_to_all(
            as_sent(spread_front(moved_signal)), "ctx", split_axis=1, concat_axis=2, tiled=True
        ),
        lax.all_to_all(
            as_sent(spread_front(moved_taps)), "ctx", split_axis=1, concat_axis=2, tiled=True
        ),
    )
    signal_spectrum = second_section(turned_signal[0], turned_signal[1], -1.0)
    filter_spectrum = second_section(turned_taps[0], turned_taps[1], -1.0)
    real_part, imag_part = spectral_product(signal_spectrum, filter_spectrum)
    real_part, imag_part = second_section(real_part, imag_part, 1.0)
    outer_index = 2 * my_index + jnp.arange(2, dtype=jnp.int32)
    real_part, imag_part = twist(
        real_part, imag_part, outer_index, jnp.arange(tok_rows, dtype=jnp.int32), padded, 1.0
    )
    returned = lax.all_to_all(
        as_sent(jnp.stack([real_part, imag_part])), "ctx", split_axis=2, concat_axis=1, tiled=True
    )
    blocks = last_section(returned[0], returned[1], shards, padded)
    convolved = (
        lax.all_to_all(as_sent(blocks), "ctx", split_axis=0, concat_axis=1, tiled=True)
        .astype(blocks.dtype)
        .reshape(tok_rows, channels)
    )
    mixed = (gate_input.astype(jnp.float32) * (convolved + skip_gain[None, :] * signal)).astype(
        jnp.bfloat16
    )
    head_count = channels // HEAD_DIM
    scale_factor = 1.0 / math.sqrt(HEAD_DIM)
    query_heads = queries.reshape(tok_rows, head_count, HEAD_DIM)
    query_pos = my_index * tok_rows + jnp.arange(tok_rows, dtype=jnp.int32)
    running_max = jnp.full((head_count, tok_rows), -1e30, jnp.float32)
    key_block = lax.all_gather(keys, "ctx", axis=0, tiled=True)
    value_block = lax.all_gather(mixed, "ctx", axis=0, tiled=True)
    key_rows = key_block.shape[0]
    key_heads = key_block.reshape(key_rows, head_count, HEAD_DIM)
    value_heads = value_block.reshape(key_rows, head_count, HEAD_DIM)
    scores = (
        jnp.einsum("qhd,khd->hqk", query_heads, key_heads, preferred_element_type=jnp.float32)
        * scale_factor
    )
    key_pos = jnp.arange(key_rows, dtype=jnp.int32)
    allowed = (key_pos[None, :] <= query_pos[:, None])[None]
    masked = jnp.where(allowed, scores, -1e30)
    newest = jnp.maximum(running_max, jnp.max(masked, axis=2))
    weights = jnp.where(allowed, jnp.exp(masked - newest[:, :, None]), 0.0)
    total_weight = jnp.sum(weights, axis=2)
    update = jnp.einsum(
        "hqk,khd->hqd",
        weights.astype(jnp.bfloat16),
        value_heads,
        preferred_element_type=jnp.float32,
    )
    accumulated = update
    running_max, total_weight, accumulated = (newest, total_weight, accumulated)
    attended = (
        (accumulated / total_weight[:, :, None])
        .transpose(1, 0, 2)
        .reshape(tok_rows, channels)
        .astype(jnp.bfloat16)
    )
    return (mixed, attended)


MESH = pl.DeviceIdType.MESH
LANES = 128
SUBLANES = 8


def split_bf16(matrix):
    high = matrix.astype(jnp.bfloat16)
    low = (matrix - high.astype(np.float64)).astype(jnp.bfloat16)
    return high, low


def block_transforms(rows):
    lags = np.arange(-rows, rows, dtype=np.int64)
    turns = (2 * np.arange(rows, dtype=np.int64)[:, None] + 1) * lags[None, :] % (4 * rows)
    angles = 2.0 * np.pi / (4 * rows) * turns
    forward = np.concatenate([np.cos(angles), -np.sin(angles)], axis=0)
    inverse = forward[:, rows:].T / rows
    return split_bf16(forward) + split_bf16(inverse)


def dot32(left, right):
    return jnp.dot(left, right, preferred_element_type=jnp.float32)


def fused_kernel(
    shards, fwd_hi, fwd_lo, inv_hi, inv_lo, skip, gate, value, taps, queries, keys,
    mixed_out, att_out,
    taps_wide, taps_sent, v_buf, t_buf, g_buf, k_buf, q_buf, v_spec, h_spec, z_spec, m_buf, a_buf,
    own_sem, in_send, in_recv, out_send, out_recv, own_out,
):
    me = lax.axis_index("ctx")
    rows = value.shape[0]
    width = v_buf.shape[1]
    heads = width // HEAD_DIM

    def partner(step):
        return lax.rem(me + step, shards)

    def block(index):
        return pl.ds(pl.multiple_of(index * rows, rows), rows)

    def columns(index, size=width, offset=0):
        return pl.ds(pl.multiple_of(index * width + offset, LANES), size)

    barrier = pltpu.get_barrier_semaphore()

    def greet(step, carry):
        pl.semaphore_signal(barrier, inc=1, device_id={"ctx": partner(step)}, device_id_type=MESH)
        return carry

    lax.fori_loop(1, shards, greet, 0)

    wide_copy = pltpu.make_async_copy(taps, taps_wide, own_out.at[0, 0])
    wide_copy.start()

    streams = [(value, v_buf, width, 0), (taps_sent, t_buf, width, 0), (gate, g_buf, width, 0)]
    for head in range(heads):
        streams.append((keys, k_buf.at[head], HEAD_DIM, head * HEAD_DIM))
        streams.append((queries, q_buf.at[head], HEAD_DIM, head * HEAD_DIM))

    def own_copy(stream):
        source, target, size, offset = streams[stream]
        return pltpu.make_async_copy(
            source.at[:, columns(me, size, offset)], target.at[block(me), :], own_sem.at[stream]
        )

    def send(stream, step):
        source, target, size, offset = streams[stream]
        peer = partner(step)
        return pltpu.make_async_remote_copy(
            src_ref=source.at[:, columns(peer, size, offset)],
            dst_ref=target.at[block(me), :],
            send_sem=in_send.at[stream, step],
            recv_sem=in_recv.at[stream, me],
            device_id={"ctx": peer},
            device_id_type=MESH,
        )

    def start_stream(stream):
        def one(step, carry):
            send(stream, step).start()
            return carry

        own_copy(stream).start()
        lax.fori_loop(1, shards, one, 0)

    def arrived(stream, step):
        target = streams[stream][1].at[block(partner(step)), :]
        pltpu.make_async_remote_copy(
            src_ref=target,
            dst_ref=target,
            send_sem=in_send.at[stream, step],
            recv_sem=in_recv.at[stream, partner(step)],
            device_id={"ctx": partner(step)},
            device_id_type=MESH,
        ).wait_recv()

    def wait_stream(stream):
        def one(step, carry):
            arrived(stream, step)
            return carry

        own_copy(stream).wait()
        lax.fori_loop(1, shards, one, 0)

    pl.semaphore_wait(barrier, shards - 1)
    start_stream(0)
    wide_copy.wait()
    taps_sent[...] = taps_wide[...].astype(jnp.bfloat16)
    for stream in range(1, len(streams)):
        start_stream(stream)

    def spectrum(index):
        signal = v_buf[block(index), :]
        v_spec[index] = dot32(fwd_hi[:, rows:], signal) + dot32(fwd_lo[:, rows:], signal)

    own_copy(0).wait()
    spectrum(me)

    def signal_step(step, carry):
        arrived(0, step)
        spectrum(partner(step))
        return carry

    lax.fori_loop(1, shards, signal_step, 0)

    wait_stream(1)
    first = t_buf[0:rows, :]
    h_spec[0] = dot32(fwd_hi[:, rows:], first) + dot32(fwd_lo[:, rows:], first)

    def taps_step(index, carry):
        window = t_buf[pl.ds(pl.multiple_of((index - 1) * rows, rows), 2 * rows), :]
        h_spec[index] = dot32(fwd_hi[...], window) + dot32(fwd_lo[...], window)
        return carry

    lax.fori_loop(1, shards, taps_step, 0)

    def product_step(chunk, carry):
        real = pl.ds(pl.multiple_of(chunk * SUBLANES, SUBLANES), SUBLANES)
        imag = pl.ds(pl.multiple_of(rows + chunk * SUBLANES, SUBLANES), SUBLANES)
        for lane in range(0, width, LANES):
            part = slice(lane, lane + LANES)
            v_real = [v_spec[i, real, part] for i in range(shards)]
            v_imag = [v_spec[i, imag, part] for i in range(shards)]
            h_real = [h_spec[i, real, part] for i in range(shards)]
            h_imag = [h_spec[i, imag, part] for i in range(shards)]
            for out in range(shards):
                total_real = v_real[0] * h_real[out] - v_imag[0] * h_imag[out]
                total_imag = v_real[0] * h_imag[out] + v_imag[0] * h_real[out]
                for i in range(1, out + 1):
                    total_real += v_real[i] * h_real[out - i] - v_imag[i] * h_imag[out - i]
                    total_imag += v_real[i] * h_imag[out - i] + v_imag[i] * h_real[out - i]
                z_spec[out, real, part] = total_real
                z_spec[out, imag, part] = total_imag
        return carry

    lax.fori_loop(0, rows // SUBLANES, product_step, 0)

    wait_stream(2)
    gain = skip[:, columns(me)]

    def mix(index):
        summed = z_spec[index]
        high = summed.astype(jnp.bfloat16)
        low = (summed - high.astype(jnp.float32)).astype(jnp.bfloat16)
        convolved = dot32(inv_hi[...], high) + dot32(inv_lo[...], high) + dot32(inv_hi[...], low)
        signal = v_buf[block(index), :].astype(jnp.float32)
        opened = g_buf[block(index), :].astype(jnp.float32)
        m_buf[block(index), :] = (opened * (convolved + gain * signal)).astype(jnp.bfloat16)

    def mixed_send(step):
        peer = partner(step)
        return pltpu.make_async_remote_copy(
            src_ref=m_buf.at[block(peer), :],
            dst_ref=mixed_out.at[:, columns(me)],
            send_sem=out_send.at[0, step],
            recv_sem=out_recv.at[0, me],
            device_id={"ctx": peer},
            device_id_type=MESH,
        )

    def mixed_own():
        return pltpu.make_async_copy(m_buf.at[block(me), :], mixed_out.at[:, columns(me)], own_out.at[0, 0])

    def mix_step(step, carry):
        mix(partner(step))
        mixed_send(step).start()
        return carry

    lax.fori_loop(1, shards, mix_step, 0)
    mix(me)
    mixed_own().start()

    scale = math.log2(math.e) / math.sqrt(HEAD_DIM)

    def att_columns(index, head):
        return pl.ds(pl.multiple_of(index * width + head * HEAD_DIM, LANES), HEAD_DIM)

    def att_send(head, step):
        peer = partner(step)
        return pltpu.make_async_remote_copy(
            src_ref=a_buf.at[head, block(peer), :],
            dst_ref=att_out.at[:, att_columns(me, head)],
            send_sem=out_send.at[1 + head, step],
            recv_sem=out_recv.at[1 + head, me],
            device_id={"ctx": peer},
            device_id_type=MESH,
        )

    def att_own(head):
        return pltpu.make_async_copy(
            a_buf.at[head, block(me), :], att_out.at[:, att_columns(me, head)], own_out.at[1, head]
        )

    def attend(head, index):
        reach = (index + 1) * rows
        scores = lax.dot_general(
            q_buf[head, index * rows : reach, :],
            k_buf[head, 0:reach, :],
            (((1,), (1,)), ((), ())),
            preferred_element_type=jnp.float32,
        )
        row = lax.broadcasted_iota(jnp.int32, (rows, rows), 0)
        column = lax.broadcasted_iota(jnp.int32, (rows, rows), 1)
        last = jnp.where(column <= row, scores[:, index * rows :], -1e30)
        if index:
            scores = jnp.concatenate([scores[:, : index * rows], last], axis=1)
        else:
            scores = last
        highest = jnp.max(scores, axis=1, keepdims=True)
        weights = jnp.exp2((scores - highest) * scale)
        total = jnp.sum(weights, axis=1, keepdims=True)
        part = slice(head * HEAD_DIM, (head + 1) * HEAD_DIM)
        update = dot32(weights.astype(jnp.bfloat16), m_buf[0:reach, part])
        a_buf[head, index * rows : reach, :] = (update / total).astype(jnp.bfloat16)

    for head in range(heads):
        wait_stream(3 + 2 * head)
        wait_stream(4 + 2 * head)

        def att_step(step, carry, head=head):
            for index in range(shards):
                @pl.when(partner(step) == index)
                def _():
                    attend(head, index)

            @pl.when(step < shards)
            def _():
                att_send(head, step).start()

            return carry

        lax.fori_loop(1, shards + 1, att_step, 0)
        att_own(head).start()

    mixed_own().wait()
    for head in range(heads):
        att_own(head).wait()

    def out_arrived(slot, target, step):
        pltpu.make_async_remote_copy(
            src_ref=target,
            dst_ref=target,
            send_sem=out_send.at[slot, step],
            recv_sem=out_recv.at[slot, partner(step)],
            device_id={"ctx": partner(step)},
            device_id_type=MESH,
        ).wait_recv()

    def finish(step, carry):
        for stream in range(len(streams)):
            send(stream, step).wait_send()
        mixed_send(step).wait_send()
        out_arrived(0, mixed_out.at[:, columns(partner(step))], step)
        for head in range(heads):
            att_send(head, step).wait_send()
            out_arrived(1 + head, att_out.at[:, att_columns(partner(step), head)], step)
        return carry

    lax.fori_loop(1, shards, finish, 0)


def by_heads(gate_input, value_input, filter_taps, skip_gain, queries, keys):
    shards = lax.axis_size("ctx")
    rows, channels = value_input.shape
    width = channels // shards
    heads = width // HEAD_DIM
    length = shards * rows
    streams = 3 + 2 * heads
    in_place = pl.BlockSpec(memory_space=pl.ANY)
    in_vmem = pl.BlockSpec(memory_space=pltpu.VMEM)
    shape = jax.ShapeDtypeStruct((rows, channels), jnp.bfloat16)
    forward_hi, forward_lo, inverse_hi, inverse_lo = block_transforms(rows)
    return pl.pallas_call(
        functools.partial(fused_kernel, shards),
        out_shape=(shape, shape),
        in_specs=[in_vmem] * 5 + [in_place] * 5,
        out_specs=(in_place, in_place),
        scratch_shapes=[
            pltpu.VMEM((rows, channels), jnp.float32),
            pltpu.VMEM((rows, channels), jnp.bfloat16),
            pltpu.VMEM((length, width), jnp.bfloat16),
            pltpu.VMEM((length, width), jnp.bfloat16),
            pltpu.VMEM((length, width), jnp.bfloat16),
            pltpu.VMEM((heads, length, HEAD_DIM), jnp.bfloat16),
            pltpu.VMEM((heads, length, HEAD_DIM), jnp.bfloat16),
            pltpu.VMEM((shards, 2 * rows, width), jnp.float32),
            pltpu.VMEM((shards, 2 * rows, width), jnp.float32),
            pltpu.VMEM((shards, 2 * rows, width), jnp.float32),
            pltpu.VMEM((length, width), jnp.bfloat16),
            pltpu.VMEM((heads, length, HEAD_DIM), jnp.bfloat16),
            pltpu.SemaphoreType.DMA((streams,)),
            pltpu.SemaphoreType.DMA((streams, shards)),
            pltpu.SemaphoreType.DMA((streams, shards)),
            pltpu.SemaphoreType.DMA((1 + heads, shards)),
            pltpu.SemaphoreType.DMA((1 + heads, shards)),
            pltpu.SemaphoreType.DMA((2, max(heads, 1))),
        ],
        compiler_params=pltpu.CompilerParams(
            collective_id=0, has_side_effects=True, vmem_limit_bytes=56 * 1024 * 1024
        ),
        name="conv_attention",
    )(
        forward_hi, forward_lo, inverse_hi, inverse_lo, skip_gain.reshape(1, channels),
        gate_input, value_input, filter_taps, queries, keys,
    )


def per_device(gate_input, value_input, filter_taps, skip_gain, queries, keys):
    shards = lax.axis_size("ctx")
    channels = value_input.shape[1]
    whole_heads = channels % (shards * HEAD_DIM) == 0
    run = by_heads if whole_heads else by_sequence
    return run(gate_input, value_input, filter_taps, skip_gain, queries, keys)


def solution(mesh):
    placed = (
        P("ctx", "tp"),
        P("ctx", "tp"),
        P("ctx", "tp"),
        P("tp"),
        P("ctx", "tp"),
        P("ctx", "tp"),
    )
    return jax.shard_map(
        per_device,
        mesh=mesh,
        in_specs=placed,
        out_specs=(P("ctx", "tp"), P("ctx", "tp")),
        check_vma=False,
    )
```

```python
import functools
import math

import jax
import jax.numpy as jnp
import numpy as np
from jax import lax
from jax.experimental import pallas as pl
from jax.experimental.pallas import tpu as pltpu
from jax.sharding import PartitionSpec as P

HEAD_DIM = 128


PRECISE = lax.Precision.HIGHEST
TWO_PI = 2.0 * math.pi


def as_sent(value):

    def short(part):
        return part.astype(jnp.bfloat16) if part.dtype == jnp.float32 else part

    return jax.tree.map(short, value)


def unit_roots(first_index, second_index, period, orient):
    product = first_index[:, None] * second_index[None, :] % period
    angles = TWO_PI / period * product.astype(jnp.float32)
    return (jnp.cos(angles), orient * jnp.sin(angles))


def first_section(signal, shards):
    cosine, sine_part = unit_roots(
        jnp.arange(2 * shards, dtype=jnp.int32),
        jnp.arange(shards, dtype=jnp.int32),
        2 * shards,
        -1.0,
    )
    real_part = jnp.einsum("kn,nmc->kmc", cosine, signal, precision=PRECISE)
    imag_part = jnp.einsum("kn,nmc->kmc", sine_part, signal, precision=PRECISE)
    return (real_part, imag_part)


def twist(real_part, imag_part, outer_index, inner_index, padded, orient):
    cosine, sine_part = unit_roots(outer_index, inner_index, padded, orient)
    cosine = cosine[:, :, None]
    sine_part = sine_part[:, :, None]
    return (real_part * cosine - imag_part * sine_part, real_part * sine_part + imag_part * cosine)


def contract(matrix, operand):
    return jnp.einsum("qn,knc->kqc", matrix, operand, precision=PRECISE)


def second_section(real_part, imag_part, orient):
    length = real_part.shape[1]
    indices = jnp.arange(length, dtype=jnp.int32)
    cosine, sine_part = unit_roots(indices, indices, length, orient)
    new_real = contract(cosine, real_part) - contract(sine_part, imag_part)
    new_imag = contract(sine_part, real_part) + contract(cosine, imag_part)
    return (new_real, new_imag)


def last_section(real_part, imag_part, shards, padded):
    cosine, sine_part = unit_roots(
        jnp.arange(shards, dtype=jnp.int32),
        jnp.arange(2 * shards, dtype=jnp.int32),
        2 * shards,
        1.0,
    )
    summed = jnp.einsum("nk,kmc->nmc", cosine, real_part, precision=PRECISE) - jnp.einsum(
        "nk,kmc->nmc", sine_part, imag_part, precision=PRECISE
    )
    return summed * (1.0 / padded)


def spectral_product(signal_spectrum, filter_spectrum):
    signal_real, signal_imag = signal_spectrum
    filter_real, filter_imag = filter_spectrum
    return (
        signal_real * filter_real - signal_imag * filter_imag,
        signal_real * filter_imag + signal_imag * filter_real,
    )


def by_sequence(gate_input, value_input, filter_taps, skip_gain, queries, keys):
    shards = lax.axis_size("ctx")
    my_index = lax.axis_index("ctx")
    tok_rows, channels = value_input.shape
    padded = 2 * shards * tok_rows
    signal = value_input.astype(jnp.float32)
    wide_index = jnp.arange(2 * shards, dtype=jnp.int32)
    slab_rows = tok_rows // shards
    moved_signal, moved_taps = (
        lax.all_to_all(
            signal.reshape(1, tok_rows, channels).astype(jnp.bfloat16),
            "ctx",
            split_axis=1,
            concat_axis=0,
            tiled=True,
        ).astype(jnp.float32),
        lax.all_to_all(
            filter_taps.reshape(1, tok_rows, channels).astype(jnp.bfloat16),
            "ctx",
            split_axis=1,
            concat_axis=0,
            tiled=True,
        ).astype(jnp.float32),
    )
    inner_index = my_index * slab_rows + jnp.arange(slab_rows, dtype=jnp.int32)

    def spread_front(block):
        real_part, imag_part = first_section(block, shards)
        real_part, imag_part = twist(real_part, imag_part, wide_index, inner_index, padded, -1.0)
        return jnp.stack([real_part, imag_part])

    turned_signal, turned_taps = (
        lax.all_to_all(
            as_sent(spread_front(moved_signal)), "ctx", split_axis=1, concat_axis=2, tiled=True
        ),
        lax.all_to_all(
            as_sent(spread_front(moved_taps)), "ctx", split_axis=1, concat_axis=2, tiled=True
        ),
    )
    signal_spectrum = second_section(turned_signal[0], turned_signal[1], -1.0)
    filter_spectrum = second_section(turned_taps[0], turned_taps[1], -1.0)
    real_part, imag_part = spectral_product(signal_spectrum, filter_spectrum)
    real_part, imag_part = second_section(real_part, imag_part, 1.0)
    outer_index = 2 * my_index + jnp.arange(2, dtype=jnp.int32)
    real_part, imag_part = twist(
        real_part, imag_part, outer_index, jnp.arange(tok_rows, dtype=jnp.int32), padded, 1.0
    )
    returned = lax.all_to_all(
        as_sent(jnp.stack([real_part, imag_part])), "ctx", split_axis=2, concat_axis=1, tiled=True
    )
    blocks = last_section(returned[0], returned[1], shards, padded)
    convolved = (
        lax.all_to_all(as_sent(blocks), "ctx", split_axis=0, concat_axis=1, tiled=True)
        .astype(blocks.dtype)
        .reshape(tok_rows, channels)
    )
    mixed = (gate_input.astype(jnp.float32) * (convolved + skip_gain[None, :] * signal)).astype(
        jnp.bfloat16
    )
    head_count = channels // HEAD_DIM
    scale_factor = 1.0 / math.sqrt(HEAD_DIM)
    query_heads = queries.reshape(tok_rows, head_count, HEAD_DIM)
    query_pos = my_index * tok_rows + jnp.arange(tok_rows, dtype=jnp.int32)
    running_max = jnp.full((head_count, tok_rows), -1e30, jnp.float32)
    key_block = lax.all_gather(keys, "ctx", axis=0, tiled=True)
    value_block = lax.all_gather(mixed, "ctx", axis=0, tiled=True)
    key_rows = key_block.shape[0]
    key_heads = key_block.reshape(key_rows, head_count, HEAD_DIM)
    value_heads = value_block.reshape(key_rows, head_count, HEAD_DIM)
    scores = (
        jnp.einsum("qhd,khd->hqk", query_heads, key_heads, preferred_element_type=jnp.float32)
        * scale_factor
    )
    key_pos = jnp.arange(key_rows, dtype=jnp.int32)
    allowed = (key_pos[None, :] <= query_pos[:, None])[None]
    masked = jnp.where(allowed, scores, -1e30)
    newest = jnp.maximum(running_max, jnp.max(masked, axis=2))
    weights = jnp.where(allowed, jnp.exp(masked - newest[:, :, None]), 0.0)
    total_weight = jnp.sum(weights, axis=2)
    update = jnp.einsum(
        "hqk,khd->hqd",
        weights.astype(jnp.bfloat16),
        value_heads,
        preferred_element_type=jnp.float32,
    )
    accumulated = update
    running_max, total_weight, accumulated = (newest, total_weight, accumulated)
    attended = (
        (accumulated / total_weight[:, :, None])
        .transpose(1, 0, 2)
        .reshape(tok_rows, channels)
        .astype(jnp.bfloat16)
    )
    return (mixed, attended)


MESH = pl.DeviceIdType.MESH
LANES = 128
SUBLANES = 8


def split_bf16(matrix):
    high = matrix.astype(jnp.bfloat16)
    low = (matrix - high.astype(np.float64)).astype(jnp.bfloat16)
    return high, low


def block_transforms(rows):
    lags = np.arange(-rows, rows, dtype=np.int64)
    turns = (2 * np.arange(rows, dtype=np.int64)[:, None] + 1) * lags[None, :] % (4 * rows)
    angles = 2.0 * np.pi / (4 * rows) * turns
    forward = np.concatenate([np.cos(angles), -np.sin(angles)], axis=0)
    inverse = forward[:, rows:].T / rows
    return split_bf16(forward) + split_bf16(inverse)


def dot32(left, right):
    return jnp.dot(left, right, preferred_element_type=jnp.float32)


def fused_kernel(
    shards, fwd_hi, fwd_lo, inv_hi, inv_lo, skip, gate, value, taps, queries, keys,
    mixed_out, att_out,
    taps_wide, taps_sent, v_buf, t_buf, g_buf, k_buf, q_buf, v_spec, h_spec, z_spec, m_buf, a_buf,
    own_sem, in_send, in_recv, out_send, out_recv, own_out,
):
    me = lax.axis_index("ctx")
    rows = value.shape[0]
    width = v_buf.shape[1]
    heads = width // HEAD_DIM

    def partner(step):
        if shards % 4:
            return lax.rem(me + step, shards)
        outer = shards // 4
        core = me % 2
        turn = step // 2
        along_x = (1 - core) * (turn % 2) + core * (turn // outer)
        along_y = (1 - core) * (turn // 2) + core * (turn % outer)
        new_core = (core + step) % 2
        new_x = (me // 2 + along_x) % 2
        new_y = (me // 4 + along_y) % outer
        return (new_y * 2 + new_x) * 2 + new_core

    def ordered(turn):
        return turn % (shards - 1) + 1 + (turn // shards) * (shards - 2)

    def block(index):
        return pl.ds(pl.multiple_of(index * rows, rows), rows)

    def columns(index, size=width, offset=0):
        return pl.ds(pl.multiple_of(index * width + offset, LANES), size)

    barrier = pltpu.get_barrier_semaphore()

    def greet(step, carry):
        pl.semaphore_signal(barrier, inc=1, device_id={"ctx": partner(step)}, device_id_type=MESH)
        return carry

    lax.fori_loop(1, shards, greet, 0)

    wide_copy = pltpu.make_async_copy(taps, taps_wide, own_out.at[0, 0])
    wide_copy.start()

    streams = [(value, v_buf, width, 0), (taps_sent, t_buf, width, 0), (gate, g_buf, width, 0)]
    for head in range(heads):
        streams.append((keys, k_buf.at[head], HEAD_DIM, head * HEAD_DIM))
        streams.append((queries, q_buf.at[head], HEAD_DIM, head * HEAD_DIM))

    def own_copy(stream):
        source, target, size, offset = streams[stream]
        return pltpu.make_async_copy(
            source.at[:, columns(me, size, offset)], target.at[block(me), :], own_sem.at[stream]
        )

    def send(stream, step):
        source, target, size, offset = streams[stream]
        peer = partner(step)
        return pltpu.make_async_remote_copy(
            src_ref=source.at[:, columns(peer, size, offset)],
            dst_ref=target.at[block(me), :],
            send_sem=in_send.at[stream, step],
            recv_sem=in_recv.at[stream, me],
            device_id={"ctx": peer},
            device_id_type=MESH,
        )

    def start_stream(stream):
        def one(turn, carry):
            send(stream, ordered(turn)).start()
            return carry

        own_copy(stream).start()
        lax.fori_loop(1, shards, one, 0)

    def arrived(stream, step):
        target = streams[stream][1].at[block(partner(step)), :]
        pltpu.make_async_remote_copy(
            src_ref=target,
            dst_ref=target,
            send_sem=in_send.at[stream, step],
            recv_sem=in_recv.at[stream, partner(step)],
            device_id={"ctx": partner(step)},
            device_id_type=MESH,
        ).wait_recv()

    def wait_stream(stream):
        def one(step, carry):
            arrived(stream, step)
            return carry

        own_copy(stream).wait()
        lax.fori_loop(1, shards, one, 0)

    pl.semaphore_wait(barrier, shards - 1)
    start_stream(0)
    wide_copy.wait()
    taps_sent[...] = taps_wide[...].astype(jnp.bfloat16)
    start_stream(1)

    def spectrum(index):
        signal = v_buf[block(index), :]
        v_spec[index] = dot32(fwd_hi[:, rows:], signal) + dot32(fwd_lo[:, rows:], signal)

    own_copy(0).wait()
    spectrum(me)

    def signal_step(turn, carry):
        step = ordered(turn)
        arrived(0, step)
        spectrum(partner(step))
        return carry

    lax.fori_loop(1, shards, signal_step, 0)

    start_stream(2)
    wait_stream(1)
    for stream in range(3, min(5, len(streams))):
        start_stream(stream)
    first = t_buf[0:rows, :]
    h_spec[0] = dot32(fwd_hi[:, rows:], first) + dot32(fwd_lo[:, rows:], first)

    def taps_step(index, carry):
        window = t_buf[pl.ds(pl.multiple_of((index - 1) * rows, rows), 2 * rows), :]
        h_spec[index] = dot32(fwd_hi[...], window) + dot32(fwd_lo[...], window)
        return carry

    lax.fori_loop(1, shards, taps_step, 0)

    def product_step(chunk, carry):
        real = pl.ds(pl.multiple_of(chunk * SUBLANES, SUBLANES), SUBLANES)
        imag = pl.ds(pl.multiple_of(rows + chunk * SUBLANES, SUBLANES), SUBLANES)
        for lane in range(0, width, LANES):
            part = slice(lane, lane + LANES)
            v_real = [v_spec[i, real, part] for i in range(shards)]
            v_imag = [v_spec[i, imag, part] for i in range(shards)]
            h_real = [h_spec[i, real, part] for i in range(shards)]
            h_imag = [h_spec[i, imag, part] for i in range(shards)]
            for out in range(shards):
                total_real = v_real[0] * h_real[out] - v_imag[0] * h_imag[out]
                total_imag = v_real[0] * h_imag[out] + v_imag[0] * h_real[out]
                for i in range(1, out + 1):
                    total_real += v_real[i] * h_real[out - i] - v_imag[i] * h_imag[out - i]
                    total_imag += v_real[i] * h_imag[out - i] + v_imag[i] * h_real[out - i]
                z_spec[out, real, part] = total_real
                z_spec[out, imag, part] = total_imag
        return carry

    lax.fori_loop(0, rows // SUBLANES, product_step, 0)

    wait_stream(2)
    for stream in range(5, len(streams)):
        start_stream(stream)
    gain = skip[:, columns(me)]

    def mix(index):
        summed = z_spec[index]
        high = summed.astype(jnp.bfloat16)
        low = (summed - high.astype(jnp.float32)).astype(jnp.bfloat16)
        convolved = dot32(inv_hi[...], high) + dot32(inv_lo[...], high) + dot32(inv_hi[...], low)
        signal = v_buf[block(index), :].astype(jnp.float32)
        opened = g_buf[block(index), :].astype(jnp.float32)
        m_buf[block(index), :] = (opened * (convolved + gain * signal)).astype(jnp.bfloat16)

    def mixed_send(step):
        peer = partner(step)
        return pltpu.make_async_remote_copy(
            src_ref=m_buf.at[block(peer), :],
            dst_ref=mixed_out.at[:, columns(me)],
            send_sem=out_send.at[0, step],
            recv_sem=out_recv.at[0, me],
            device_id={"ctx": peer},
            device_id_type=MESH,
        )

    def mixed_own():
        return pltpu.make_async_copy(m_buf.at[block(me), :], mixed_out.at[:, columns(me)], own_out.at[0, 0])

    def mix_step(turn, carry):
        step = ordered(turn)
        mix(partner(step))
        mixed_send(step).start()
        return carry

    lax.fori_loop(1, shards, mix_step, 0)
    mix(me)
    mixed_own().start()

    scale = math.log2(math.e) / math.sqrt(HEAD_DIM)

    def att_columns(index, head):
        return pl.ds(pl.multiple_of(index * width + head * HEAD_DIM, LANES), HEAD_DIM)

    def att_send(head, step):
        peer = partner(step)
        return pltpu.make_async_remote_copy(
            src_ref=a_buf.at[head, block(peer), :],
            dst_ref=att_out.at[:, att_columns(me, head)],
            send_sem=out_send.at[1 + head, step],
            recv_sem=out_recv.at[1 + head, me],
            device_id={"ctx": peer},
            device_id_type=MESH,
        )

    def att_own(head):
        return pltpu.make_async_copy(
            a_buf.at[head, block(me), :], att_out.at[:, att_columns(me, head)], own_out.at[1, head]
        )

    def attend(head, index):
        reach = (index + 1) * rows
        scores = lax.dot_general(
            q_buf[head, index * rows : reach, :],
            k_buf[head, 0:reach, :],
            (((1,), (1,)), ((), ())),
            preferred_element_type=jnp.float32,
        )
        row = lax.broadcasted_iota(jnp.int32, (rows, rows), 0)
        column = lax.broadcasted_iota(jnp.int32, (rows, rows), 1)
        last = jnp.where(column <= row, scores[:, index * rows :], -1e30)
        if index:
            scores = jnp.concatenate([scores[:, : index * rows], last], axis=1)
        else:
            scores = last
        highest = jnp.max(scores, axis=1, keepdims=True)
        weights = jnp.exp2((scores - highest) * scale)
        total = jnp.sum(weights, axis=1, keepdims=True)
        part = slice(head * HEAD_DIM, (head + 1) * HEAD_DIM)
        update = dot32(weights.astype(jnp.bfloat16), m_buf[0:reach, part])
        a_buf[head, index * rows : reach, :] = (update / total).astype(jnp.bfloat16)

    for head in range(heads):
        wait_stream(3 + 2 * head)
        wait_stream(4 + 2 * head)

        def att_step(turn, carry, head=head):
            step = ordered(turn)
            for index in range(shards):
                @pl.when(partner(step) == index)
                def _():
                    attend(head, index)

            @pl.when(turn < shards)
            def _():
                att_send(head, step).start()

            return carry

        lax.fori_loop(1, shards + 1, att_step, 0)
        att_own(head).start()

    mixed_own().wait()
    for head in range(heads):
        att_own(head).wait()

    def out_arrived(slot, target, step):
        pltpu.make_async_remote_copy(
            src_ref=target,
            dst_ref=target,
            send_sem=out_send.at[slot, step],
            recv_sem=out_recv.at[slot, partner(step)],
            device_id={"ctx": partner(step)},
            device_id_type=MESH,
        ).wait_recv()

    def finish(step, carry):
        for stream in range(len(streams)):
            send(stream, step).wait_send()
        mixed_send(step).wait_send()
        out_arrived(0, mixed_out.at[:, columns(partner(step))], step)
        for head in range(heads):
            att_send(head, step).wait_send()
            out_arrived(1 + head, att_out.at[:, att_columns(partner(step), head)], step)
        return carry

    lax.fori_loop(1, shards, finish, 0)


def by_heads(gate_input, value_input, filter_taps, skip_gain, queries, keys):
    shards = lax.axis_size("ctx")
    rows, channels = value_input.shape
    width = channels // shards
    heads = width // HEAD_DIM
    length = shards * rows
    streams = 3 + 2 * heads
    in_place = pl.BlockSpec(memory_space=pl.ANY)
    in_vmem = pl.BlockSpec(memory_space=pltpu.VMEM)
    shape = jax.ShapeDtypeStruct((rows, channels), jnp.bfloat16)
    forward_hi, forward_lo, inverse_hi, inverse_lo = block_transforms(rows)
    return pl.pallas_call(
        functools.partial(fused_kernel, shards),
        out_shape=(shape, shape),
        in_specs=[in_vmem] * 5 + [in_place] * 5,
        out_specs=(in_place, in_place),
        scratch_shapes=[
            pltpu.VMEM((rows, channels), jnp.float32),
            pltpu.VMEM((rows, channels), jnp.bfloat16),
            pltpu.VMEM((length, width), jnp.bfloat16),
            pltpu.VMEM((length, width), jnp.bfloat16),
            pltpu.VMEM((length, width), jnp.bfloat16),
            pltpu.VMEM((heads, length, HEAD_DIM), jnp.bfloat16),
            pltpu.VMEM((heads, length, HEAD_DIM), jnp.bfloat16),
            pltpu.VMEM((shards, 2 * rows, width), jnp.float32),
            pltpu.VMEM((shards, 2 * rows, width), jnp.float32),
            pltpu.VMEM((shards, 2 * rows, width), jnp.float32),
            pltpu.VMEM((length, width), jnp.bfloat16),
            pltpu.VMEM((heads, length, HEAD_DIM), jnp.bfloat16),
            pltpu.SemaphoreType.DMA((streams,)),
            pltpu.SemaphoreType.DMA((streams, shards)),
            pltpu.SemaphoreType.DMA((streams, shards)),
            pltpu.SemaphoreType.DMA((1 + heads, shards)),
            pltpu.SemaphoreType.DMA((1 + heads, shards)),
            pltpu.SemaphoreType.DMA((2, max(heads, 1))),
        ],
        compiler_params=pltpu.CompilerParams(
            collective_id=0, has_side_effects=True, vmem_limit_bytes=56 * 1024 * 1024
        ),
        name="conv_attention",
    )(
        forward_hi, forward_lo, inverse_hi, inverse_lo, skip_gain.reshape(1, channels),
        gate_input, value_input, filter_taps, queries, keys,
    )


def per_device(gate_input, value_input, filter_taps, skip_gain, queries, keys):
    shards = lax.axis_size("ctx")
    channels = value_input.shape[1]
    whole_heads = channels % (shards * HEAD_DIM) == 0
    run = by_heads if whole_heads else by_sequence
    return run(gate_input, value_input, filter_taps, skip_gain, queries, keys)


def solution(mesh):
    placed = (
        P("ctx", "tp"),
        P("ctx", "tp"),
        P("ctx", "tp"),
        P("tp"),
        P("ctx", "tp"),
        P("ctx", "tp"),
    )
    return jax.shard_map(
        per_device,
        mesh=mesh,
        in_specs=placed,
        out_specs=(P("ctx", "tp"), P("ctx", "tp")),
        check_vma=False,
    )
```

```python
import functools
import math

import jax
import jax.numpy as jnp
import numpy as np
from jax import lax
from jax.experimental import pallas as pl
from jax.experimental.pallas import tpu as pltpu
from jax.sharding import PartitionSpec as P

HEAD_DIM = 128


PRECISE = lax.Precision.HIGHEST
TWO_PI = 2.0 * math.pi


def as_sent(value):

    def short(part):
        return part.astype(jnp.bfloat16) if part.dtype == jnp.float32 else part

    return jax.tree.map(short, value)


def unit_roots(first_index, second_index, period, orient):
    product = first_index[:, None] * second_index[None, :] % period
    angles = TWO_PI / period * product.astype(jnp.float32)
    return (jnp.cos(angles), orient * jnp.sin(angles))


def first_section(signal, shards):
    cosine, sine_part = unit_roots(
        jnp.arange(2 * shards, dtype=jnp.int32),
        jnp.arange(shards, dtype=jnp.int32),
        2 * shards,
        -1.0,
    )
    real_part = jnp.einsum("kn,nmc->kmc", cosine, signal, precision=PRECISE)
    imag_part = jnp.einsum("kn,nmc->kmc", sine_part, signal, precision=PRECISE)
    return (real_part, imag_part)


def twist(real_part, imag_part, outer_index, inner_index, padded, orient):
    cosine, sine_part = unit_roots(outer_index, inner_index, padded, orient)
    cosine = cosine[:, :, None]
    sine_part = sine_part[:, :, None]
    return (real_part * cosine - imag_part * sine_part, real_part * sine_part + imag_part * cosine)


def contract(matrix, operand):
    return jnp.einsum("qn,knc->kqc", matrix, operand, precision=PRECISE)


def second_section(real_part, imag_part, orient):
    length = real_part.shape[1]
    indices = jnp.arange(length, dtype=jnp.int32)
    cosine, sine_part = unit_roots(indices, indices, length, orient)
    new_real = contract(cosine, real_part) - contract(sine_part, imag_part)
    new_imag = contract(sine_part, real_part) + contract(cosine, imag_part)
    return (new_real, new_imag)


def last_section(real_part, imag_part, shards, padded):
    cosine, sine_part = unit_roots(
        jnp.arange(shards, dtype=jnp.int32),
        jnp.arange(2 * shards, dtype=jnp.int32),
        2 * shards,
        1.0,
    )
    summed = jnp.einsum("nk,kmc->nmc", cosine, real_part, precision=PRECISE) - jnp.einsum(
        "nk,kmc->nmc", sine_part, imag_part, precision=PRECISE
    )
    return summed * (1.0 / padded)


def spectral_product(signal_spectrum, filter_spectrum):
    signal_real, signal_imag = signal_spectrum
    filter_real, filter_imag = filter_spectrum
    return (
        signal_real * filter_real - signal_imag * filter_imag,
        signal_real * filter_imag + signal_imag * filter_real,
    )


def by_sequence(gate_input, value_input, filter_taps, skip_gain, queries, keys):
    shards = lax.axis_size("ctx")
    my_index = lax.axis_index("ctx")
    tok_rows, channels = value_input.shape
    padded = 2 * shards * tok_rows
    signal = value_input.astype(jnp.float32)
    wide_index = jnp.arange(2 * shards, dtype=jnp.int32)
    slab_rows = tok_rows // shards
    moved_signal, moved_taps = (
        lax.all_to_all(
            signal.reshape(1, tok_rows, channels).astype(jnp.bfloat16),
            "ctx",
            split_axis=1,
            concat_axis=0,
            tiled=True,
        ).astype(jnp.float32),
        lax.all_to_all(
            filter_taps.reshape(1, tok_rows, channels).astype(jnp.bfloat16),
            "ctx",
            split_axis=1,
            concat_axis=0,
            tiled=True,
        ).astype(jnp.float32),
    )
    inner_index = my_index * slab_rows + jnp.arange(slab_rows, dtype=jnp.int32)

    def spread_front(block):
        real_part, imag_part = first_section(block, shards)
        real_part, imag_part = twist(real_part, imag_part, wide_index, inner_index, padded, -1.0)
        return jnp.stack([real_part, imag_part])

    turned_signal, turned_taps = (
        lax.all_to_all(
            as_sent(spread_front(moved_signal)), "ctx", split_axis=1, concat_axis=2, tiled=True
        ),
        lax.all_to_all(
            as_sent(spread_front(moved_taps)), "ctx", split_axis=1, concat_axis=2, tiled=True
        ),
    )
    signal_spectrum = second_section(turned_signal[0], turned_signal[1], -1.0)
    filter_spectrum = second_section(turned_taps[0], turned_taps[1], -1.0)
    real_part, imag_part = spectral_product(signal_spectrum, filter_spectrum)
    real_part, imag_part = second_section(real_part, imag_part, 1.0)
    outer_index = 2 * my_index + jnp.arange(2, dtype=jnp.int32)
    real_part, imag_part = twist(
        real_part, imag_part, outer_index, jnp.arange(tok_rows, dtype=jnp.int32), padded, 1.0
    )
    returned = lax.all_to_all(
        as_sent(jnp.stack([real_part, imag_part])), "ctx", split_axis=2, concat_axis=1, tiled=True
    )
    blocks = last_section(returned[0], returned[1], shards, padded)
    convolved = (
        lax.all_to_all(as_sent(blocks), "ctx", split_axis=0, concat_axis=1, tiled=True)
        .astype(blocks.dtype)
        .reshape(tok_rows, channels)
    )
    mixed = (gate_input.astype(jnp.float32) * (convolved + skip_gain[None, :] * signal)).astype(
        jnp.bfloat16
    )
    head_count = channels // HEAD_DIM
    scale_factor = 1.0 / math.sqrt(HEAD_DIM)
    query_heads = queries.reshape(tok_rows, head_count, HEAD_DIM)
    query_pos = my_index * tok_rows + jnp.arange(tok_rows, dtype=jnp.int32)
    running_max = jnp.full((head_count, tok_rows), -1e30, jnp.float32)
    key_block = lax.all_gather(keys, "ctx", axis=0, tiled=True)
    value_block = lax.all_gather(mixed, "ctx", axis=0, tiled=True)
    key_rows = key_block.shape[0]
    key_heads = key_block.reshape(key_rows, head_count, HEAD_DIM)
    value_heads = value_block.reshape(key_rows, head_count, HEAD_DIM)
    scores = (
        jnp.einsum("qhd,khd->hqk", query_heads, key_heads, preferred_element_type=jnp.float32)
        * scale_factor
    )
    key_pos = jnp.arange(key_rows, dtype=jnp.int32)
    allowed = (key_pos[None, :] <= query_pos[:, None])[None]
    masked = jnp.where(allowed, scores, -1e30)
    newest = jnp.maximum(running_max, jnp.max(masked, axis=2))
    weights = jnp.where(allowed, jnp.exp(masked - newest[:, :, None]), 0.0)
    total_weight = jnp.sum(weights, axis=2)
    update = jnp.einsum(
        "hqk,khd->hqd",
        weights.astype(jnp.bfloat16),
        value_heads,
        preferred_element_type=jnp.float32,
    )
    accumulated = update
    running_max, total_weight, accumulated = (newest, total_weight, accumulated)
    attended = (
        (accumulated / total_weight[:, :, None])
        .transpose(1, 0, 2)
        .reshape(tok_rows, channels)
        .astype(jnp.bfloat16)
    )
    return (mixed, attended)


MESH = pl.DeviceIdType.MESH
LANES = 128
SUBLANES = 8


def split_bf16(matrix):
    high = matrix.astype(jnp.bfloat16)
    low = (matrix - high.astype(np.float64)).astype(jnp.bfloat16)
    return high, low


def block_transforms(rows):
    lags = np.arange(-rows, rows, dtype=np.int64)
    turns = (2 * np.arange(rows, dtype=np.int64)[:, None] + 1) * lags[None, :] % (4 * rows)
    angles = 2.0 * np.pi / (4 * rows) * turns
    forward = np.concatenate([np.cos(angles), -np.sin(angles)], axis=0)
    inverse = forward[:, rows:].T / rows
    return split_bf16(forward) + split_bf16(inverse)


def dot32(left, right):
    return jnp.dot(left, right, preferred_element_type=jnp.float32)


def fused_kernel(
    shards, fwd_hi, fwd_lo, inv_hi, inv_lo, skip, gate, value, taps, queries, keys,
    mixed_out, att_out,
    taps_wide, taps_sent, v_buf, t_buf, g_buf, k_buf, q_buf, v_spec, h_spec, z_spec, m_buf, a_buf,
    s_buf, p_buf, l_buf,
    own_sem, in_send, in_recv, out_send, out_recv, own_out,
):
    me = lax.axis_index("ctx")
    rows = value.shape[0]
    width = v_buf.shape[1]
    heads = width // HEAD_DIM

    def partner(step):
        if shards % 4:
            return lax.rem(me + step, shards)
        outer = shards // 4
        core = me % 2
        turn = step // 2
        along_x = (1 - core) * (turn % 2) + core * (turn // outer)
        along_y = (1 - core) * (turn // 2) + core * (turn % outer)
        new_core = (core + step) % 2
        new_x = (me // 2 + along_x) % 2
        new_y = (me // 4 + along_y) % outer
        return (new_y * 2 + new_x) * 2 + new_core

    def ordered(turn):
        return turn % (shards - 1) + 1 + (turn // shards) * (shards - 2)

    def block(index):
        return pl.ds(pl.multiple_of(index * rows, rows), rows)

    def columns(index, size=width, offset=0):
        return pl.ds(pl.multiple_of(index * width + offset, LANES), size)

    barrier = pltpu.get_barrier_semaphore()

    def greet(step, carry):
        pl.semaphore_signal(barrier, inc=1, device_id={"ctx": partner(step)}, device_id_type=MESH)
        return carry

    lax.fori_loop(1, shards, greet, 0)

    wide_copy = pltpu.make_async_copy(taps, taps_wide, own_out.at[0, 0])
    wide_copy.start()

    streams = [(value, v_buf, width, 0), (taps_sent, t_buf, width, 0), (gate, g_buf, width, 0)]
    for head in range(heads):
        streams.append((keys, k_buf.at[head], HEAD_DIM, head * HEAD_DIM))
        streams.append((queries, q_buf.at[head], HEAD_DIM, head * HEAD_DIM))

    def own_copy(stream):
        source, target, size, offset = streams[stream]
        return pltpu.make_async_copy(
            source.at[:, columns(me, size, offset)], target.at[block(me), :], own_sem.at[stream]
        )

    def send(stream, step):
        source, target, size, offset = streams[stream]
        peer = partner(step)
        return pltpu.make_async_remote_copy(
            src_ref=source.at[:, columns(peer, size, offset)],
            dst_ref=target.at[block(me), :],
            send_sem=in_send.at[stream, step],
            recv_sem=in_recv.at[stream, me],
            device_id={"ctx": peer},
            device_id_type=MESH,
        )

    def start_stream(stream):
        def one(turn, carry):
            send(stream, ordered(turn)).start()
            return carry

        own_copy(stream).start()
        lax.fori_loop(1, shards, one, 0)

    def arrived(stream, step):
        target = streams[stream][1].at[block(partner(step)), :]
        pltpu.make_async_remote_copy(
            src_ref=target,
            dst_ref=target,
            send_sem=in_send.at[stream, step],
            recv_sem=in_recv.at[stream, partner(step)],
            device_id={"ctx": partner(step)},
            device_id_type=MESH,
        ).wait_recv()

    def wait_stream(stream):
        def one(step, carry):
            arrived(stream, step)
            return carry

        own_copy(stream).wait()
        lax.fori_loop(1, shards, one, 0)

    pl.semaphore_wait(barrier, shards - 1)
    start_stream(0)
    wide_copy.wait()
    taps_sent[...] = taps_wide[...].astype(jnp.bfloat16)
    start_stream(1)

    def spectrum(index):
        signal = v_buf[block(index), :]
        v_spec[index] = dot32(fwd_hi[:, rows:], signal) + dot32(fwd_lo[:, rows:], signal)

    own_copy(0).wait()
    spectrum(me)

    def signal_step(turn, carry):
        step = ordered(turn)
        arrived(0, step)
        spectrum(partner(step))
        return carry

    lax.fori_loop(1, shards, signal_step, 0)

    start_stream(2)
    wait_stream(1)
    for stream in range(3, min(5, len(streams))):
        start_stream(stream)
    first = t_buf[0:rows, :]
    h_spec[0] = dot32(fwd_hi[:, rows:], first) + dot32(fwd_lo[:, rows:], first)

    def taps_step(index, carry):
        window = t_buf[pl.ds(pl.multiple_of((index - 1) * rows, rows), 2 * rows), :]
        h_spec[index] = dot32(fwd_hi[...], window) + dot32(fwd_lo[...], window)
        return carry

    lax.fori_loop(1, shards, taps_step, 0)

    def product_step(chunk, carry):
        real = pl.ds(pl.multiple_of(chunk * SUBLANES, SUBLANES), SUBLANES)
        imag = pl.ds(pl.multiple_of(rows + chunk * SUBLANES, SUBLANES), SUBLANES)
        for lane in range(0, width, LANES):
            part = slice(lane, lane + LANES)
            v_real = [v_spec[i, real, part] for i in range(shards)]
            v_imag = [v_spec[i, imag, part] for i in range(shards)]
            h_real = [h_spec[i, real, part] for i in range(shards)]
            h_imag = [h_spec[i, imag, part] for i in range(shards)]
            for out in range(shards):
                total_real = v_real[0] * h_real[out] - v_imag[0] * h_imag[out]
                total_imag = v_real[0] * h_imag[out] + v_imag[0] * h_real[out]
                for i in range(1, out + 1):
                    total_real += v_real[i] * h_real[out - i] - v_imag[i] * h_imag[out - i]
                    total_imag += v_real[i] * h_imag[out - i] + v_imag[i] * h_real[out - i]
                z_spec[out, real, part] = total_real
                z_spec[out, imag, part] = total_imag
        return carry

    lax.fori_loop(0, rows // SUBLANES, product_step, 0)

    wait_stream(2)
    for stream in range(5, len(streams)):
        start_stream(stream)
    gain = skip[:, columns(me)]

    def mix(index):
        summed = z_spec[index]
        high = summed.astype(jnp.bfloat16)
        low = (summed - high.astype(jnp.float32)).astype(jnp.bfloat16)
        convolved = dot32(inv_hi[...], high) + dot32(inv_lo[...], high) + dot32(inv_hi[...], low)
        signal = v_buf[block(index), :].astype(jnp.float32)
        opened = g_buf[block(index), :].astype(jnp.float32)
        m_buf[block(index), :] = (opened * (convolved + gain * signal)).astype(jnp.bfloat16)

    def mixed_send(step):
        peer = partner(step)
        return pltpu.make_async_remote_copy(
            src_ref=m_buf.at[block(peer), :],
            dst_ref=mixed_out.at[:, columns(me)],
            send_sem=out_send.at[0, step],
            recv_sem=out_recv.at[0, me],
            device_id={"ctx": peer},
            device_id_type=MESH,
        )

    def mixed_own():
        return pltpu.make_async_copy(m_buf.at[block(me), :], mixed_out.at[:, columns(me)], own_out.at[0, 0])

    def mix_step(turn, carry):
        step = ordered(turn)
        mix(partner(step))
        mixed_send(step).start()
        return carry

    lax.fori_loop(1, shards, mix_step, 0)
    mix(me)
    mixed_own().start()

    scale = math.log2(math.e) / math.sqrt(HEAD_DIM)

    def att_columns(index, head):
        return pl.ds(pl.multiple_of(index * width + head * HEAD_DIM, LANES), HEAD_DIM)

    def att_send(head, step):
        peer = partner(step)
        return pltpu.make_async_remote_copy(
            src_ref=a_buf.at[head, block(peer), :],
            dst_ref=att_out.at[:, att_columns(me, head)],
            send_sem=out_send.at[1 + head, step],
            recv_sem=out_recv.at[1 + head, me],
            device_id={"ctx": peer},
            device_id_type=MESH,
        )

    def att_own(head):
        return pltpu.make_async_copy(
            a_buf.at[head, block(me), :], att_out.at[:, att_columns(me, head)], own_out.at[1, head]
        )

    def attend(head, index):
        reach = (index + 1) * rows
        before = index * rows
        s_buf[:, 0:reach] = lax.dot_general(
            q_buf[head, before:reach, :],
            k_buf[head, 0:reach, :],
            (((1,), (1,)), ((), ())),
            preferred_element_type=jnp.float32,
        )
        tile = 16 if reach > 4 * rows else 32

        def softmax_tile(turn, carry):
            span = pl.ds(pl.multiple_of(turn * tile, tile), tile)
            row = lax.broadcasted_iota(jnp.int32, (tile, rows), 0) + turn * tile
            column = lax.broadcasted_iota(jnp.int32, (tile, rows), 1)
            last = jnp.where(column <= row, s_buf[span, before:reach], -1e30)
            highest = jnp.max(last, axis=1, keepdims=True)
            if index:
                early = s_buf[span, 0:before]
                highest = jnp.maximum(highest, jnp.max(early, axis=1, keepdims=True))
            top = highest * scale
            last = jnp.exp2(last * scale - top)
            total = jnp.sum(last, axis=1, keepdims=True)
            p_buf[span, before:reach] = last.astype(jnp.bfloat16)
            if index:
                early = jnp.exp2(early * scale - top)
                total += jnp.sum(early, axis=1, keepdims=True)
                p_buf[span, 0:before] = early.astype(jnp.bfloat16)
            l_buf[span, :] = jnp.broadcast_to(total, (tile, HEAD_DIM))
            return carry

        lax.fori_loop(0, rows // tile, softmax_tile, 0, unroll=2)
        part = slice(head * HEAD_DIM, (head + 1) * HEAD_DIM)
        update = dot32(p_buf[:, 0:reach], m_buf[0:reach, part])
        a_buf[head, before:reach, :] = (update / l_buf[...]).astype(jnp.bfloat16)

    for head in range(heads):
        wait_stream(3 + 2 * head)
        wait_stream(4 + 2 * head)

        def att_step(turn, carry, head=head):
            step = ordered(turn)
            for index in range(shards):
                @pl.when(partner(step) == index)
                def _():
                    attend(head, index)

            @pl.when(turn < shards)
            def _():
                att_send(head, step).start()

            return carry

        lax.fori_loop(1, shards + 1, att_step, 0)
        att_own(head).start()

    mixed_own().wait()
    for head in range(heads):
        att_own(head).wait()

    def out_arrived(slot, target, step):
        pltpu.make_async_remote_copy(
            src_ref=target,
            dst_ref=target,
            send_sem=out_send.at[slot, step],
            recv_sem=out_recv.at[slot, partner(step)],
            device_id={"ctx": partner(step)},
            device_id_type=MESH,
        ).wait_recv()

    def finish(step, carry):
        for stream in range(len(streams)):
            send(stream, step).wait_send()
        mixed_send(step).wait_send()
        out_arrived(0, mixed_out.at[:, columns(partner(step))], step)
        for head in range(heads):
            att_send(head, step).wait_send()
            out_arrived(1 + head, att_out.at[:, att_columns(partner(step), head)], step)
        return carry

    lax.fori_loop(1, shards, finish, 0)


def by_heads(gate_input, value_input, filter_taps, skip_gain, queries, keys):
    shards = lax.axis_size("ctx")
    rows, channels = value_input.shape
    width = channels // shards
    heads = width // HEAD_DIM
    length = shards * rows
    streams = 3 + 2 * heads
    in_place = pl.BlockSpec(memory_space=pl.ANY)
    in_vmem = pl.BlockSpec(memory_space=pltpu.VMEM)
    shape = jax.ShapeDtypeStruct((rows, channels), jnp.bfloat16)
    forward_hi, forward_lo, inverse_hi, inverse_lo = block_transforms(rows)
    results = pl.pallas_call(
        functools.partial(fused_kernel, shards),
        out_shape=(shape, shape),
        in_specs=[in_vmem] * 5 + [in_place] * 5,
        out_specs=(in_place, in_place),
        scratch_shapes=[
            pltpu.VMEM((rows, channels), jnp.float32),
            pltpu.VMEM((rows, channels), jnp.bfloat16),
            pltpu.VMEM((length, width), jnp.bfloat16),
            pltpu.VMEM((length, width), jnp.bfloat16),
            pltpu.VMEM((length, width), jnp.bfloat16),
            pltpu.VMEM((heads, length, HEAD_DIM), jnp.bfloat16),
            pltpu.VMEM((heads, length, HEAD_DIM), jnp.bfloat16),
            pltpu.VMEM((shards, 2 * rows, width), jnp.float32),
            pltpu.VMEM((shards, 2 * rows, width), jnp.float32),
            pltpu.VMEM((shards, 2 * rows, width), jnp.float32),
            pltpu.VMEM((length, width), jnp.bfloat16),
            pltpu.VMEM((heads, length, HEAD_DIM), jnp.bfloat16),
            pltpu.VMEM((rows, length), jnp.float32),
            pltpu.VMEM((rows, length), jnp.bfloat16),
            pltpu.VMEM((rows, HEAD_DIM), jnp.float32),
            pltpu.SemaphoreType.DMA((streams,)),
            pltpu.SemaphoreType.DMA((streams, shards)),
            pltpu.SemaphoreType.DMA((streams, shards)),
            pltpu.SemaphoreType.DMA((1 + heads, shards)),
            pltpu.SemaphoreType.DMA((1 + heads, shards)),
            pltpu.SemaphoreType.DMA((2, max(heads, 1))),
        ],
        compiler_params=pltpu.CompilerParams(
            collective_id=0, has_side_effects=True, vmem_limit_bytes=56 * 1024 * 1024
        ),
        name="conv_attention",
    )(
        forward_hi, forward_lo, inverse_hi, inverse_lo, skip_gain.reshape(1, channels),
        gate_input, value_input, filter_taps, queries, keys,
    )
    return pl.pallas_call(
        hand_over,
        out_shape=(shape, shape),
        in_specs=[in_place] * 2,
        out_specs=(in_place, in_place),
        scratch_shapes=[pltpu.SemaphoreType.DMA((2, HAND_OVERS))],
        compiler_params=pltpu.CompilerParams(vmem_limit_bytes=56 * 1024 * 1024),
        name="hand_over",
    )(*results)


HAND_OVERS = 4


def hand_over(first, second, first_out, second_out, sems):
    rows = first.shape[0] // HAND_OVERS
    copies = []
    for number, (source, target) in enumerate(((first, first_out), (second, second_out))):
        for part in range(HAND_OVERS):
            span = pl.ds(part * rows, rows)
            copies.append(pltpu.make_async_copy(source.at[span, :], target.at[span, :], sems.at[number, part]))
    for copy in copies:
        copy.start()
    for copy in copies:
        copy.wait()


def per_device(gate_input, value_input, filter_taps, skip_gain, queries, keys):
    shards = lax.axis_size("ctx")
    channels = value_input.shape[1]
    whole_heads = channels % (shards * HEAD_DIM) == 0
    run = by_heads if whole_heads else by_sequence
    return run(gate_input, value_input, filter_taps, skip_gain, queries, keys)


def solution(mesh):
    placed = (
        P("ctx", "tp"),
        P("ctx", "tp"),
        P("ctx", "tp"),
        P("tp"),
        P("ctx", "tp"),
        P("ctx", "tp"),
    )
    return jax.shard_map(
        per_device,
        mesh=mesh,
        in_specs=placed,
        out_specs=(P("ctx", "tp"), P("ctx", "tp")),
        check_vma=False,
    )
```

```python
import functools
import math

import jax
import jax.numpy as jnp
import numpy as np
from jax import lax
from jax.experimental import pallas as pl
from jax.experimental.pallas import tpu as pltpu
from jax.sharding import PartitionSpec as P

HEAD_DIM = 128


PRECISE = lax.Precision.HIGHEST
TWO_PI = 2.0 * math.pi


def as_sent(value):

    def short(part):
        return part.astype(jnp.bfloat16) if part.dtype == jnp.float32 else part

    return jax.tree.map(short, value)


def unit_roots(first_index, second_index, period, orient):
    product = first_index[:, None] * second_index[None, :] % period
    angles = TWO_PI / period * product.astype(jnp.float32)
    return (jnp.cos(angles), orient * jnp.sin(angles))


def first_section(signal, shards):
    cosine, sine_part = unit_roots(
        jnp.arange(2 * shards, dtype=jnp.int32),
        jnp.arange(shards, dtype=jnp.int32),
        2 * shards,
        -1.0,
    )
    real_part = jnp.einsum("kn,nmc->kmc", cosine, signal, precision=PRECISE)
    imag_part = jnp.einsum("kn,nmc->kmc", sine_part, signal, precision=PRECISE)
    return (real_part, imag_part)


def twist(real_part, imag_part, outer_index, inner_index, padded, orient):
    cosine, sine_part = unit_roots(outer_index, inner_index, padded, orient)
    cosine = cosine[:, :, None]
    sine_part = sine_part[:, :, None]
    return (real_part * cosine - imag_part * sine_part, real_part * sine_part + imag_part * cosine)


def contract(matrix, operand):
    return jnp.einsum("qn,knc->kqc", matrix, operand, precision=PRECISE)


def second_section(real_part, imag_part, orient):
    length = real_part.shape[1]
    indices = jnp.arange(length, dtype=jnp.int32)
    cosine, sine_part = unit_roots(indices, indices, length, orient)
    new_real = contract(cosine, real_part) - contract(sine_part, imag_part)
    new_imag = contract(sine_part, real_part) + contract(cosine, imag_part)
    return (new_real, new_imag)


def last_section(real_part, imag_part, shards, padded):
    cosine, sine_part = unit_roots(
        jnp.arange(shards, dtype=jnp.int32),
        jnp.arange(2 * shards, dtype=jnp.int32),
        2 * shards,
        1.0,
    )
    summed = jnp.einsum("nk,kmc->nmc", cosine, real_part, precision=PRECISE) - jnp.einsum(
        "nk,kmc->nmc", sine_part, imag_part, precision=PRECISE
    )
    return summed * (1.0 / padded)


def spectral_product(signal_spectrum, filter_spectrum):
    signal_real, signal_imag = signal_spectrum
    filter_real, filter_imag = filter_spectrum
    return (
        signal_real * filter_real - signal_imag * filter_imag,
        signal_real * filter_imag + signal_imag * filter_real,
    )


def by_sequence(gate_input, value_input, filter_taps, skip_gain, queries, keys):
    shards = lax.axis_size("ctx")
    my_index = lax.axis_index("ctx")
    tok_rows, channels = value_input.shape
    padded = 2 * shards * tok_rows
    signal = value_input.astype(jnp.float32)
    wide_index = jnp.arange(2 * shards, dtype=jnp.int32)
    slab_rows = tok_rows // shards
    moved_signal, moved_taps = (
        lax.all_to_all(
            signal.reshape(1, tok_rows, channels).astype(jnp.bfloat16),
            "ctx",
            split_axis=1,
            concat_axis=0,
            tiled=True,
        ).astype(jnp.float32),
        lax.all_to_all(
            filter_taps.reshape(1, tok_rows, channels).astype(jnp.bfloat16),
            "ctx",
            split_axis=1,
            concat_axis=0,
            tiled=True,
        ).astype(jnp.float32),
    )
    inner_index = my_index * slab_rows + jnp.arange(slab_rows, dtype=jnp.int32)

    def spread_front(block):
        real_part, imag_part = first_section(block, shards)
        real_part, imag_part = twist(real_part, imag_part, wide_index, inner_index, padded, -1.0)
        return jnp.stack([real_part, imag_part])

    turned_signal, turned_taps = (
        lax.all_to_all(
            as_sent(spread_front(moved_signal)), "ctx", split_axis=1, concat_axis=2, tiled=True
        ),
        lax.all_to_all(
            as_sent(spread_front(moved_taps)), "ctx", split_axis=1, concat_axis=2, tiled=True
        ),
    )
    signal_spectrum = second_section(turned_signal[0], turned_signal[1], -1.0)
    filter_spectrum = second_section(turned_taps[0], turned_taps[1], -1.0)
    real_part, imag_part = spectral_product(signal_spectrum, filter_spectrum)
    real_part, imag_part = second_section(real_part, imag_part, 1.0)
    outer_index = 2 * my_index + jnp.arange(2, dtype=jnp.int32)
    real_part, imag_part = twist(
        real_part, imag_part, outer_index, jnp.arange(tok_rows, dtype=jnp.int32), padded, 1.0
    )
    returned = lax.all_to_all(
        as_sent(jnp.stack([real_part, imag_part])), "ctx", split_axis=2, concat_axis=1, tiled=True
    )
    blocks = last_section(returned[0], returned[1], shards, padded)
    convolved = (
        lax.all_to_all(as_sent(blocks), "ctx", split_axis=0, concat_axis=1, tiled=True)
        .astype(blocks.dtype)
        .reshape(tok_rows, channels)
    )
    mixed = (gate_input.astype(jnp.float32) * (convolved + skip_gain[None, :] * signal)).astype(
        jnp.bfloat16
    )
    head_count = channels // HEAD_DIM
    scale_factor = 1.0 / math.sqrt(HEAD_DIM)
    query_heads = queries.reshape(tok_rows, head_count, HEAD_DIM)
    query_pos = my_index * tok_rows + jnp.arange(tok_rows, dtype=jnp.int32)
    running_max = jnp.full((head_count, tok_rows), -1e30, jnp.float32)
    key_block = lax.all_gather(keys, "ctx", axis=0, tiled=True)
    value_block = lax.all_gather(mixed, "ctx", axis=0, tiled=True)
    key_rows = key_block.shape[0]
    key_heads = key_block.reshape(key_rows, head_count, HEAD_DIM)
    value_heads = value_block.reshape(key_rows, head_count, HEAD_DIM)
    scores = (
        jnp.einsum("qhd,khd->hqk", query_heads, key_heads, preferred_element_type=jnp.float32)
        * scale_factor
    )
    key_pos = jnp.arange(key_rows, dtype=jnp.int32)
    allowed = (key_pos[None, :] <= query_pos[:, None])[None]
    masked = jnp.where(allowed, scores, -1e30)
    newest = jnp.maximum(running_max, jnp.max(masked, axis=2))
    weights = jnp.where(allowed, jnp.exp(masked - newest[:, :, None]), 0.0)
    total_weight = jnp.sum(weights, axis=2)
    update = jnp.einsum(
        "hqk,khd->hqd",
        weights.astype(jnp.bfloat16),
        value_heads,
        preferred_element_type=jnp.float32,
    )
    accumulated = update
    running_max, total_weight, accumulated = (newest, total_weight, accumulated)
    attended = (
        (accumulated / total_weight[:, :, None])
        .transpose(1, 0, 2)
        .reshape(tok_rows, channels)
        .astype(jnp.bfloat16)
    )
    return (mixed, attended)


MESH = pl.DeviceIdType.MESH
LANES = 128
SUBLANES = 8


def split_bf16(matrix):
    high = matrix.astype(jnp.bfloat16)
    low = (matrix - high.astype(np.float64)).astype(jnp.bfloat16)
    return high, low


def block_transforms(rows):
    lags = np.arange(-rows, rows, dtype=np.int64)
    turns = (2 * np.arange(rows, dtype=np.int64)[:, None] + 1) * lags[None, :] % (4 * rows)
    angles = 2.0 * np.pi / (4 * rows) * turns
    forward = np.concatenate([np.cos(angles), -np.sin(angles)], axis=0)
    inverse = forward[:, rows:].T / rows
    return split_bf16(forward) + split_bf16(inverse)


def dot32(left, right):
    return jnp.dot(left, right, preferred_element_type=jnp.float32)


def fused_kernel(
    shards, fwd_hi, fwd_lo, inv_hi, inv_lo, skip, gate, value, taps, queries, keys,
    mixed_out, att_out,
    taps_wide, taps_sent, v_buf, t_buf, g_buf, k_buf, q_buf, v_spec, h_spec, z_spec, m_buf, a_buf,
    s_buf, p_buf, l_buf, v_sent, g_sent, k_sent, q_sent, mixed_in, att_in,
    own_sem, in_send, in_recv, out_send, out_recv, own_out, stage_sem, end_sem,
):
    me = lax.axis_index("ctx")
    rows = value.shape[0]
    width = v_buf.shape[1]
    heads = width // HEAD_DIM

    def partner(step):
        if shards % 4:
            return lax.rem(me + step, shards)
        outer = shards // 4
        core = me % 2
        turn = step // 2
        along_x = (1 - core) * (turn % 2) + core * (turn // outer)
        along_y = (1 - core) * (turn // 2) + core * (turn % outer)
        new_core = (core + step) % 2
        new_x = (me // 2 + along_x) % 2
        new_y = (me // 4 + along_y) % outer
        return (new_y * 2 + new_x) * 2 + new_core

    def ordered(turn):
        return turn % (shards - 1) + 1 + (turn // shards) * (shards - 2)

    def block(index):
        return pl.ds(pl.multiple_of(index * rows, rows), rows)

    def columns(index, size=width, offset=0):
        return pl.ds(pl.multiple_of(index * width + offset, LANES), size)

    barrier = pltpu.get_barrier_semaphore()

    def greet(step, carry):
        pl.semaphore_signal(barrier, inc=1, device_id={"ctx": partner(step)}, device_id_type=MESH)
        return carry

    lax.fori_loop(1, shards, greet, 0)

    wide_copy = pltpu.make_async_copy(taps, taps_wide, own_out.at[0, 0])
    staged = [
        pltpu.make_async_copy(source, target, stage_sem.at[number])
        for number, (source, target) in enumerate(
            ((value, v_sent), (gate, g_sent), (keys, k_sent), (queries, q_sent))
        )
    ]
    staged[0].start()
    wide_copy.start()
    for copy in staged[1:]:
        copy.start()

    streams = [(v_sent, v_buf, width, 0), (taps_sent, t_buf, width, 0), (g_sent, g_buf, width, 0)]
    for head in range(heads):
        streams.append((k_sent, k_buf.at[head], HEAD_DIM, head * HEAD_DIM))
        streams.append((q_sent, q_buf.at[head], HEAD_DIM, head * HEAD_DIM))

    def own_copy(stream):
        source, target, size, offset = streams[stream]
        return pltpu.make_async_copy(
            source.at[:, columns(me, size, offset)], target.at[block(me), :], own_sem.at[stream]
        )

    def send(stream, step):
        source, target, size, offset = streams[stream]
        peer = partner(step)
        return pltpu.make_async_remote_copy(
            src_ref=source.at[:, columns(peer, size, offset)],
            dst_ref=target.at[block(me), :],
            send_sem=in_send.at[stream, step],
            recv_sem=in_recv.at[stream, me],
            device_id={"ctx": peer},
            device_id_type=MESH,
        )

    def start_stream(stream):
        def one(turn, carry):
            send(stream, ordered(turn)).start()
            return carry

        own_copy(stream).start()
        lax.fori_loop(1, shards, one, 0)

    def arrived(stream, step):
        target = streams[stream][1].at[block(partner(step)), :]
        pltpu.make_async_remote_copy(
            src_ref=target,
            dst_ref=target,
            send_sem=in_send.at[stream, step],
            recv_sem=in_recv.at[stream, partner(step)],
            device_id={"ctx": partner(step)},
            device_id_type=MESH,
        ).wait_recv()

    def wait_stream(stream):
        def one(step, carry):
            arrived(stream, step)
            return carry

        own_copy(stream).wait()
        lax.fori_loop(1, shards, one, 0)

    pl.semaphore_wait(barrier, shards - 1)
    staged[0].wait()
    start_stream(0)
    wide_copy.wait()
    taps_sent[...] = taps_wide[...].astype(jnp.bfloat16)
    start_stream(1)

    def spectrum(index):
        signal = v_buf[block(index), :]
        v_spec[index] = dot32(fwd_hi[:, rows:], signal) + dot32(fwd_lo[:, rows:], signal)

    own_copy(0).wait()
    spectrum(me)

    def signal_step(turn, carry):
        step = ordered(turn)
        arrived(0, step)
        spectrum(partner(step))
        return carry

    lax.fori_loop(1, shards, signal_step, 0)

    staged[1].wait()
    start_stream(2)
    wait_stream(1)
    staged[2].wait()
    staged[3].wait()
    for stream in range(3, min(5, len(streams))):
        start_stream(stream)
    first = t_buf[0:rows, :]
    h_spec[0] = dot32(fwd_hi[:, rows:], first) + dot32(fwd_lo[:, rows:], first)

    def taps_step(index, carry):
        window = t_buf[pl.ds(pl.multiple_of((index - 1) * rows, rows), 2 * rows), :]
        h_spec[index] = dot32(fwd_hi[...], window) + dot32(fwd_lo[...], window)
        return carry

    lax.fori_loop(1, shards, taps_step, 0)

    def product_step(chunk, carry):
        real = pl.ds(pl.multiple_of(chunk * SUBLANES, SUBLANES), SUBLANES)
        imag = pl.ds(pl.multiple_of(rows + chunk * SUBLANES, SUBLANES), SUBLANES)
        for lane in range(0, width, LANES):
            part = slice(lane, lane + LANES)
            v_real = [v_spec[i, real, part] for i in range(shards)]
            v_imag = [v_spec[i, imag, part] for i in range(shards)]
            h_real = [h_spec[i, real, part] for i in range(shards)]
            h_imag = [h_spec[i, imag, part] for i in range(shards)]
            for out in range(shards):
                total_real = v_real[0] * h_real[out] - v_imag[0] * h_imag[out]
                total_imag = v_real[0] * h_imag[out] + v_imag[0] * h_real[out]
                for i in range(1, out + 1):
                    total_real += v_real[i] * h_real[out - i] - v_imag[i] * h_imag[out - i]
                    total_imag += v_real[i] * h_imag[out - i] + v_imag[i] * h_real[out - i]
                z_spec[out, real, part] = total_real
                z_spec[out, imag, part] = total_imag
        return carry

    lax.fori_loop(0, rows // SUBLANES, product_step, 0)

    wait_stream(2)
    for stream in range(5, len(streams)):
        start_stream(stream)
    gain = skip[:, columns(me)]

    def mix(index):
        summed = z_spec[index]
        high = summed.astype(jnp.bfloat16)
        low = (summed - high.astype(jnp.float32)).astype(jnp.bfloat16)
        convolved = dot32(inv_hi[...], high) + dot32(inv_lo[...], high) + dot32(inv_hi[...], low)
        signal = v_buf[block(index), :].astype(jnp.float32)
        opened = g_buf[block(index), :].astype(jnp.float32)
        m_buf[block(index), :] = (opened * (convolved + gain * signal)).astype(jnp.bfloat16)

    def mixed_send(step):
        peer = partner(step)
        return pltpu.make_async_remote_copy(
            src_ref=m_buf.at[block(peer), :],
            dst_ref=mixed_in.at[:, columns(me)],
            send_sem=out_send.at[0, step],
            recv_sem=out_recv.at[0, me],
            device_id={"ctx": peer},
            device_id_type=MESH,
        )

    def mixed_own():
        return pltpu.make_async_copy(m_buf.at[block(me), :], mixed_in.at[:, columns(me)], own_out.at[0, 0])

    def mix_step(turn, carry):
        step = ordered(turn)
        mix(partner(step))
        mixed_send(step).start()
        return carry

    lax.fori_loop(1, shards, mix_step, 0)
    mix(me)
    mixed_own().start()

    scale = math.log2(math.e) / math.sqrt(HEAD_DIM)

    def att_columns(index, head):
        return pl.ds(pl.multiple_of(index * width + head * HEAD_DIM, LANES), HEAD_DIM)

    def att_send(head, step):
        peer = partner(step)
        return pltpu.make_async_remote_copy(
            src_ref=a_buf.at[head, block(peer), :],
            dst_ref=att_in.at[:, att_columns(me, head)],
            send_sem=out_send.at[1 + head, step],
            recv_sem=out_recv.at[1 + head, me],
            device_id={"ctx": peer},
            device_id_type=MESH,
        )

    def att_own(head):
        return pltpu.make_async_copy(
            a_buf.at[head, block(me), :], att_in.at[:, att_columns(me, head)], own_out.at[1, head]
        )

    def attend(head, index):
        reach = (index + 1) * rows
        before = index * rows
        s_buf[:, 0:reach] = lax.dot_general(
            q_buf[head, before:reach, :],
            k_buf[head, 0:reach, :],
            (((1,), (1,)), ((), ())),
            preferred_element_type=jnp.float32,
        )
        tile = 16 if reach > 4 * rows else 32

        def softmax_tile(turn, carry):
            span = pl.ds(pl.multiple_of(turn * tile, tile), tile)
            row = lax.broadcasted_iota(jnp.int32, (tile, rows), 0) + turn * tile
            column = lax.broadcasted_iota(jnp.int32, (tile, rows), 1)
            last = jnp.where(column <= row, s_buf[span, before:reach], -1e30)
            highest = jnp.max(last, axis=1, keepdims=True)
            if index:
                early = s_buf[span, 0:before]
                highest = jnp.maximum(highest, jnp.max(early, axis=1, keepdims=True))
            top = highest * scale
            last = jnp.exp2(last * scale - top)
            total = jnp.sum(last, axis=1, keepdims=True)
            p_buf[span, before:reach] = last.astype(jnp.bfloat16)
            if index:
                early = jnp.exp2(early * scale - top)
                total += jnp.sum(early, axis=1, keepdims=True)
                p_buf[span, 0:before] = early.astype(jnp.bfloat16)
            l_buf[span, :] = jnp.broadcast_to(total, (tile, HEAD_DIM))
            return carry

        lax.fori_loop(0, rows // tile, softmax_tile, 0, unroll=2)
        part = slice(head * HEAD_DIM, (head + 1) * HEAD_DIM)
        update = dot32(p_buf[:, 0:reach], m_buf[0:reach, part])
        a_buf[head, before:reach, :] = (update / l_buf[...]).astype(jnp.bfloat16)

    for head in range(heads):
        wait_stream(3 + 2 * head)
        wait_stream(4 + 2 * head)

        def att_step(turn, carry, head=head):
            step = ordered(turn)
            for index in range(shards):
                @pl.when(partner(step) == index)
                def _():
                    attend(head, index)

            @pl.when(turn < shards)
            def _():
                att_send(head, step).start()

            return carry

        lax.fori_loop(1, shards + 1, att_step, 0)
        att_own(head).start()

    mixed_own().wait()
    for head in range(heads):
        att_own(head).wait()

    def out_arrived(slot, target, step):
        pltpu.make_async_remote_copy(
            src_ref=target,
            dst_ref=target,
            send_sem=out_send.at[slot, step],
            recv_sem=out_recv.at[slot, partner(step)],
            device_id={"ctx": partner(step)},
            device_id_type=MESH,
        ).wait_recv()

    def mixed_finish(step, carry):
        out_arrived(0, mixed_in.at[:, columns(partner(step))], step)
        return carry

    lax.fori_loop(1, shards, mixed_finish, 0)
    mixed_end = pltpu.make_async_copy(mixed_in, mixed_out, end_sem.at[0])
    mixed_end.start()

    def finish(step, carry):
        for stream in range(len(streams)):
            send(stream, step).wait_send()
        mixed_send(step).wait_send()
        for head in range(heads):
            att_send(head, step).wait_send()
            out_arrived(1 + head, att_in.at[:, att_columns(partner(step), head)], step)
        return carry

    lax.fori_loop(1, shards, finish, 0)
    att_end = pltpu.make_async_copy(att_in, att_out, end_sem.at[1])
    att_end.start()
    mixed_end.wait()
    att_end.wait()


def by_heads(gate_input, value_input, filter_taps, skip_gain, queries, keys):
    shards = lax.axis_size("ctx")
    rows, channels = value_input.shape
    width = channels // shards
    heads = width // HEAD_DIM
    length = shards * rows
    streams = 3 + 2 * heads
    in_place = pl.BlockSpec(memory_space=pl.ANY)
    in_vmem = pl.BlockSpec(memory_space=pltpu.VMEM)
    shape = jax.ShapeDtypeStruct((rows, channels), jnp.bfloat16)
    forward_hi, forward_lo, inverse_hi, inverse_lo = block_transforms(rows)
    results = pl.pallas_call(
        functools.partial(fused_kernel, shards),
        out_shape=(shape, shape),
        in_specs=[in_vmem] * 5 + [in_place] * 5,
        out_specs=(in_place, in_place),
        scratch_shapes=[
            pltpu.VMEM((rows, channels), jnp.float32),
            pltpu.VMEM((rows, channels), jnp.bfloat16),
            pltpu.VMEM((length, width), jnp.bfloat16),
            pltpu.VMEM((length, width), jnp.bfloat16),
            pltpu.VMEM((length, width), jnp.bfloat16),
            pltpu.VMEM((heads, length, HEAD_DIM), jnp.bfloat16),
            pltpu.VMEM((heads, length, HEAD_DIM), jnp.bfloat16),
            pltpu.VMEM((shards, 2 * rows, width), jnp.float32),
            pltpu.VMEM((shards, 2 * rows, width), jnp.float32),
            pltpu.VMEM((shards, 2 * rows, width), jnp.float32),
            pltpu.VMEM((length, width), jnp.bfloat16),
            pltpu.VMEM((heads, length, HEAD_DIM), jnp.bfloat16),
            pltpu.VMEM((rows, length), jnp.float32),
            pltpu.VMEM((rows, length), jnp.bfloat16),
            pltpu.VMEM((rows, HEAD_DIM), jnp.float32),
        ]
        + [pltpu.VMEM((rows, channels), jnp.bfloat16)] * 6
        + [
            pltpu.SemaphoreType.DMA((streams,)),
            pltpu.SemaphoreType.DMA((streams, shards)),
            pltpu.SemaphoreType.DMA((streams, shards)),
            pltpu.SemaphoreType.DMA((1 + heads, shards)),
            pltpu.SemaphoreType.DMA((1 + heads, shards)),
            pltpu.SemaphoreType.DMA((2, max(heads, 1))),
            pltpu.SemaphoreType.DMA((4,)),
            pltpu.SemaphoreType.DMA((2,)),
        ],
        compiler_params=pltpu.CompilerParams(
            collective_id=0, has_side_effects=True, vmem_limit_bytes=56 * 1024 * 1024
        ),
        name="conv_attention",
    )(
        forward_hi, forward_lo, inverse_hi, inverse_lo, skip_gain.reshape(1, channels),
        gate_input, value_input, filter_taps, queries, keys,
    )
    return pl.pallas_call(
        hand_over,
        out_shape=(shape, shape),
        in_specs=[in_place] * 2,
        out_specs=(in_place, in_place),
        scratch_shapes=[pltpu.VMEM((2, rows, channels), jnp.bfloat16)]
        + [pltpu.SemaphoreType.DMA((2, HAND_OVERS))] * 2,
        compiler_params=pltpu.CompilerParams(vmem_limit_bytes=56 * 1024 * 1024),
        name="hand_over",
    )(*results)


HAND_OVERS = 4


def hand_over(first, second, first_out, second_out, held, in_sems, out_sems):
    rows = first.shape[0] // HAND_OVERS
    arriving, leaving = [], []
    for part in range(HAND_OVERS):
        span = pl.ds(part * rows, rows)
        for number, (source, target) in enumerate(((first, first_out), (second, second_out))):
            slot = held.at[number, span, :]
            arriving.append(pltpu.make_async_copy(source.at[span, :], slot, in_sems.at[number, part]))
            leaving.append(pltpu.make_async_copy(slot, target.at[span, :], out_sems.at[number, part]))
    for copy in arriving:
        copy.start()
    for copy, onward in zip(arriving, leaving):
        copy.wait()
        onward.start()
    for copy in leaving:
        copy.wait()


def per_device(gate_input, value_input, filter_taps, skip_gain, queries, keys):
    shards = lax.axis_size("ctx")
    channels = value_input.shape[1]
    whole_heads = channels % (shards * HEAD_DIM) == 0
    run = by_heads if whole_heads else by_sequence
    return run(gate_input, value_input, filter_taps, skip_gain, queries, keys)


def solution(mesh):
    placed = (
        P("ctx", "tp"),
        P("ctx", "tp"),
        P("ctx", "tp"),
        P("tp"),
        P("ctx", "tp"),
        P("ctx", "tp"),
    )
    return jax.shard_map(
        per_device,
        mesh=mesh,
        in_specs=placed,
        out_specs=(P("ctx", "tp"), P("ctx", "tp")),
        check_vma=False,
    )
```

```python
import functools
import math

import jax
import jax.numpy as jnp
import numpy as np
from jax import lax
from jax.experimental import pallas as pl
from jax.experimental.pallas import tpu as pltpu
from jax.sharding import PartitionSpec as P

HEAD_DIM = 128


PRECISE = lax.Precision.HIGHEST
TWO_PI = 2.0 * math.pi


def as_sent(value):

    def short(part):
        return part.astype(jnp.bfloat16) if part.dtype == jnp.float32 else part

    return jax.tree.map(short, value)


def unit_roots(first_index, second_index, period, orient):
    product = first_index[:, None] * second_index[None, :] % period
    angles = TWO_PI / period * product.astype(jnp.float32)
    return (jnp.cos(angles), orient * jnp.sin(angles))


def first_section(signal, shards):
    cosine, sine_part = unit_roots(
        jnp.arange(2 * shards, dtype=jnp.int32),
        jnp.arange(shards, dtype=jnp.int32),
        2 * shards,
        -1.0,
    )
    real_part = jnp.einsum("kn,nmc->kmc", cosine, signal, precision=PRECISE)
    imag_part = jnp.einsum("kn,nmc->kmc", sine_part, signal, precision=PRECISE)
    return (real_part, imag_part)


def twist(real_part, imag_part, outer_index, inner_index, padded, orient):
    cosine, sine_part = unit_roots(outer_index, inner_index, padded, orient)
    cosine = cosine[:, :, None]
    sine_part = sine_part[:, :, None]
    return (real_part * cosine - imag_part * sine_part, real_part * sine_part + imag_part * cosine)


def contract(matrix, operand):
    return jnp.einsum("qn,knc->kqc", matrix, operand, precision=PRECISE)


def second_section(real_part, imag_part, orient):
    length = real_part.shape[1]
    indices = jnp.arange(length, dtype=jnp.int32)
    cosine, sine_part = unit_roots(indices, indices, length, orient)
    new_real = contract(cosine, real_part) - contract(sine_part, imag_part)
    new_imag = contract(sine_part, real_part) + contract(cosine, imag_part)
    return (new_real, new_imag)


def last_section(real_part, imag_part, shards, padded):
    cosine, sine_part = unit_roots(
        jnp.arange(shards, dtype=jnp.int32),
        jnp.arange(2 * shards, dtype=jnp.int32),
        2 * shards,
        1.0,
    )
    summed = jnp.einsum("nk,kmc->nmc", cosine, real_part, precision=PRECISE) - jnp.einsum(
        "nk,kmc->nmc", sine_part, imag_part, precision=PRECISE
    )
    return summed * (1.0 / padded)


def spectral_product(signal_spectrum, filter_spectrum):
    signal_real, signal_imag = signal_spectrum
    filter_real, filter_imag = filter_spectrum
    return (
        signal_real * filter_real - signal_imag * filter_imag,
        signal_real * filter_imag + signal_imag * filter_real,
    )


def by_sequence(gate_input, value_input, filter_taps, skip_gain, queries, keys):
    shards = lax.axis_size("ctx")
    my_index = lax.axis_index("ctx")
    tok_rows, channels = value_input.shape
    padded = 2 * shards * tok_rows
    signal = value_input.astype(jnp.float32)
    wide_index = jnp.arange(2 * shards, dtype=jnp.int32)
    slab_rows = tok_rows // shards
    moved_signal, moved_taps = (
        lax.all_to_all(
            signal.reshape(1, tok_rows, channels).astype(jnp.bfloat16),
            "ctx",
            split_axis=1,
            concat_axis=0,
            tiled=True,
        ).astype(jnp.float32),
        lax.all_to_all(
            filter_taps.reshape(1, tok_rows, channels).astype(jnp.bfloat16),
            "ctx",
            split_axis=1,
            concat_axis=0,
            tiled=True,
        ).astype(jnp.float32),
    )
    inner_index = my_index * slab_rows + jnp.arange(slab_rows, dtype=jnp.int32)

    def spread_front(block):
        real_part, imag_part = first_section(block, shards)
        real_part, imag_part = twist(real_part, imag_part, wide_index, inner_index, padded, -1.0)
        return jnp.stack([real_part, imag_part])

    turned_signal, turned_taps = (
        lax.all_to_all(
            as_sent(spread_front(moved_signal)), "ctx", split_axis=1, concat_axis=2, tiled=True
        ),
        lax.all_to_all(
            as_sent(spread_front(moved_taps)), "ctx", split_axis=1, concat_axis=2, tiled=True
        ),
    )
    signal_spectrum = second_section(turned_signal[0], turned_signal[1], -1.0)
    filter_spectrum = second_section(turned_taps[0], turned_taps[1], -1.0)
    real_part, imag_part = spectral_product(signal_spectrum, filter_spectrum)
    real_part, imag_part = second_section(real_part, imag_part, 1.0)
    outer_index = 2 * my_index + jnp.arange(2, dtype=jnp.int32)
    real_part, imag_part = twist(
        real_part, imag_part, outer_index, jnp.arange(tok_rows, dtype=jnp.int32), padded, 1.0
    )
    returned = lax.all_to_all(
        as_sent(jnp.stack([real_part, imag_part])), "ctx", split_axis=2, concat_axis=1, tiled=True
    )
    blocks = last_section(returned[0], returned[1], shards, padded)
    convolved = (
        lax.all_to_all(as_sent(blocks), "ctx", split_axis=0, concat_axis=1, tiled=True)
        .astype(blocks.dtype)
        .reshape(tok_rows, channels)
    )
    mixed = (gate_input.astype(jnp.float32) * (convolved + skip_gain[None, :] * signal)).astype(
        jnp.bfloat16
    )
    head_count = channels // HEAD_DIM
    scale_factor = 1.0 / math.sqrt(HEAD_DIM)
    query_heads = queries.reshape(tok_rows, head_count, HEAD_DIM)
    query_pos = my_index * tok_rows + jnp.arange(tok_rows, dtype=jnp.int32)
    running_max = jnp.full((head_count, tok_rows), -1e30, jnp.float32)
    key_block = lax.all_gather(keys, "ctx", axis=0, tiled=True)
    value_block = lax.all_gather(mixed, "ctx", axis=0, tiled=True)
    key_rows = key_block.shape[0]
    key_heads = key_block.reshape(key_rows, head_count, HEAD_DIM)
    value_heads = value_block.reshape(key_rows, head_count, HEAD_DIM)
    scores = (
        jnp.einsum("qhd,khd->hqk", query_heads, key_heads, preferred_element_type=jnp.float32)
        * scale_factor
    )
    key_pos = jnp.arange(key_rows, dtype=jnp.int32)
    allowed = (key_pos[None, :] <= query_pos[:, None])[None]
    masked = jnp.where(allowed, scores, -1e30)
    newest = jnp.maximum(running_max, jnp.max(masked, axis=2))
    weights = jnp.where(allowed, jnp.exp(masked - newest[:, :, None]), 0.0)
    total_weight = jnp.sum(weights, axis=2)
    update = jnp.einsum(
        "hqk,khd->hqd",
        weights.astype(jnp.bfloat16),
        value_heads,
        preferred_element_type=jnp.float32,
    )
    accumulated = update
    running_max, total_weight, accumulated = (newest, total_weight, accumulated)
    attended = (
        (accumulated / total_weight[:, :, None])
        .transpose(1, 0, 2)
        .reshape(tok_rows, channels)
        .astype(jnp.bfloat16)
    )
    return (mixed, attended)


MESH = pl.DeviceIdType.MESH
LANES = 128
SUBLANES = 8


def split_bf16(matrix):
    high = matrix.astype(jnp.bfloat16)
    low = (matrix - high.astype(np.float64)).astype(jnp.bfloat16)
    return high, low


def block_transforms(rows):
    lags = np.arange(-rows, rows, dtype=np.int64)
    turns = (2 * np.arange(rows, dtype=np.int64)[:, None] + 1) * lags[None, :] % (4 * rows)
    angles = 2.0 * np.pi / (4 * rows) * turns
    forward = np.concatenate([np.cos(angles), -np.sin(angles)], axis=0)
    inverse = forward[:, rows:].T / rows
    return split_bf16(forward) + split_bf16(inverse)


def dot32(left, right):
    return jnp.dot(left, right, preferred_element_type=jnp.float32)


def fused_kernel(
    shards, fwd_hi_in, fwd_lo_in, inv_hi_in, inv_lo_in, skip_in, gate, value, taps, queries, keys,
    mixed_in, att_in,
    taps_wide, taps_sent, v_buf, t_buf, g_buf, k_buf, q_buf, v_spec, h_spec, z_spec, m_buf, a_buf,
    s_buf, p_buf, l_buf, fwd_hi, fwd_lo, inv_hi, inv_lo, skip,
    own_sem, in_send, in_recv, out_send, out_recv, own_out, stage_sem,
):
    me = lax.axis_index("ctx")
    rows = value.shape[0]
    width = v_buf.shape[1]
    heads = width // HEAD_DIM

    def partner(step):
        if shards % 4:
            return lax.rem(me + step, shards)
        outer = shards // 4
        core = me % 2
        turn = step // 2
        along_x = (1 - core) * (turn % 2) + core * (turn // outer)
        along_y = (1 - core) * (turn // 2) + core * (turn % outer)
        new_core = (core + step) % 2
        new_x = (me // 2 + along_x) % 2
        new_y = (me // 4 + along_y) % outer
        return (new_y * 2 + new_x) * 2 + new_core

    def ordered(turn):
        return turn % (shards - 1) + 1 + (turn // shards) * (shards - 2)

    def block(index):
        return pl.ds(pl.multiple_of(index * rows, rows), rows)

    def columns(index):
        return pl.ds(pl.multiple_of(index * width, LANES), width)

    barrier = pltpu.get_barrier_semaphore()

    def greet(step, carry):
        pl.semaphore_signal(barrier, inc=1, device_id={"ctx": partner(step)}, device_id_type=MESH)
        return carry

    lax.fori_loop(1, shards, greet, 0)

    wide_copy = pltpu.make_async_copy(taps, taps_wide, own_out.at[0])
    wide_copy.start()
    staged = [
        pltpu.make_async_copy(source, target, stage_sem.at[number])
        for number, (source, target) in enumerate(
            (
                (fwd_hi_in, fwd_hi), (fwd_lo_in, fwd_lo), (skip_in, skip),
                (inv_hi_in, inv_hi), (inv_lo_in, inv_lo),
            )
        )
    ]
    streams = [(value, v_buf), (taps_sent, t_buf), (gate, g_buf), (keys, k_buf), (queries, q_buf)]

    def own_copy(stream):
        source, target = streams[stream]
        return pltpu.make_async_copy(
            source.at[:, columns(me)], target.at[block(me), :], own_sem.at[stream]
        )

    def send(stream, step):
        source, target = streams[stream]
        peer = partner(step)
        return pltpu.make_async_remote_copy(
            src_ref=source.at[:, columns(peer)],
            dst_ref=target.at[block(me), :],
            send_sem=in_send.at[stream, step],
            recv_sem=in_recv.at[stream, me],
            device_id={"ctx": peer},
            device_id_type=MESH,
        )

    def start_stream(stream):
        def one(turn, carry):
            send(stream, ordered(turn)).start()
            return carry

        own_copy(stream).start()
        lax.fori_loop(1, shards, one, 0)

    def arrived(stream, step):
        target = streams[stream][1].at[block(partner(step)), :]
        pltpu.make_async_remote_copy(
            src_ref=target,
            dst_ref=target,
            send_sem=in_send.at[stream, step],
            recv_sem=in_recv.at[stream, partner(step)],
            device_id={"ctx": partner(step)},
            device_id_type=MESH,
        ).wait_recv()

    def wait_stream(stream):
        def one(step, carry):
            arrived(stream, step)
            return carry

        own_copy(stream).wait()
        lax.fori_loop(1, shards, one, 0)

    pl.semaphore_wait(barrier, shards - 1)
    start_stream(0)
    for copy in staged:
        copy.start()
    wide_copy.wait()
    taps_sent[...] = taps_wide[...].astype(jnp.bfloat16)
    start_stream(1)

    def spectrum(index):
        signal = v_buf[block(index), :]
        v_spec[index] = dot32(fwd_hi[:, rows:], signal) + dot32(fwd_lo[:, rows:], signal)

    for copy in staged:
        copy.wait()
    own_copy(0).wait()
    spectrum(me)

    def signal_step(turn, carry):
        step = ordered(turn)
        arrived(0, step)
        spectrum(partner(step))
        return carry

    lax.fori_loop(1, shards, signal_step, 0)

    start_stream(2)
    wait_stream(1)
    start_stream(3)
    start_stream(4)
    first = t_buf[0:rows, :]
    h_spec[0] = dot32(fwd_hi[:, rows:], first) + dot32(fwd_lo[:, rows:], first)

    def taps_step(index, carry):
        window = t_buf[pl.ds(pl.multiple_of((index - 1) * rows, rows), 2 * rows), :]
        h_spec[index] = dot32(fwd_hi[...], window) + dot32(fwd_lo[...], window)
        return carry

    lax.fori_loop(1, shards, taps_step, 0)

    def product_step(chunk, carry):
        real = pl.ds(pl.multiple_of(chunk * SUBLANES, SUBLANES), SUBLANES)
        imag = pl.ds(pl.multiple_of(rows + chunk * SUBLANES, SUBLANES), SUBLANES)
        for lane in range(0, width, LANES):
            part = slice(lane, lane + LANES)
            v_real = [v_spec[i, real, part] for i in range(shards)]
            v_imag = [v_spec[i, imag, part] for i in range(shards)]
            h_real = [h_spec[i, real, part] for i in range(shards)]
            h_imag = [h_spec[i, imag, part] for i in range(shards)]
            for out in range(shards):
                total_real = v_real[0] * h_real[out] - v_imag[0] * h_imag[out]
                total_imag = v_real[0] * h_imag[out] + v_imag[0] * h_real[out]
                for i in range(1, out + 1):
                    total_real += v_real[i] * h_real[out - i] - v_imag[i] * h_imag[out - i]
                    total_imag += v_real[i] * h_imag[out - i] + v_imag[i] * h_real[out - i]
                z_spec[out, real, part] = total_real
                z_spec[out, imag, part] = total_imag
        return carry

    lax.fori_loop(0, rows // SUBLANES, product_step, 0)

    wait_stream(2)
    gain = skip[:, columns(me)]

    def mix(index):
        summed = z_spec[index]
        high = summed.astype(jnp.bfloat16)
        low = (summed - high.astype(jnp.float32)).astype(jnp.bfloat16)
        convolved = dot32(inv_hi[...], high) + dot32(inv_lo[...], high) + dot32(inv_hi[...], low)
        signal = v_buf[block(index), :].astype(jnp.float32)
        opened = g_buf[block(index), :].astype(jnp.float32)
        m_buf[block(index), :] = (opened * (convolved + gain * signal)).astype(jnp.bfloat16)

    def mixed_send(step):
        peer = partner(step)
        return pltpu.make_async_remote_copy(
            src_ref=m_buf.at[block(peer), :],
            dst_ref=mixed_in.at[:, columns(me)],
            send_sem=out_send.at[0, step],
            recv_sem=out_recv.at[0, me],
            device_id={"ctx": peer},
            device_id_type=MESH,
        )

    def mixed_own():
        return pltpu.make_async_copy(m_buf.at[block(me), :], mixed_in.at[:, columns(me)], own_out.at[0])

    def mix_step(turn, carry):
        step = ordered(turn)
        mix(partner(step))
        mixed_send(step).start()
        return carry

    lax.fori_loop(1, shards, mix_step, 0)
    mix(me)
    mixed_own().start()

    scale = math.log2(math.e) / math.sqrt(HEAD_DIM)

    def att_send(step):
        peer = partner(step)
        return pltpu.make_async_remote_copy(
            src_ref=a_buf.at[block(peer), :],
            dst_ref=att_in.at[:, columns(me)],
            send_sem=out_send.at[1, step],
            recv_sem=out_recv.at[1, me],
            device_id={"ctx": peer},
            device_id_type=MESH,
        )

    def att_own():
        return pltpu.make_async_copy(a_buf.at[block(me), :], att_in.at[:, columns(me)], own_out.at[1])

    def attend(head, index):
        reach = (index + 1) * rows
        before = index * rows
        part = slice(head * HEAD_DIM, (head + 1) * HEAD_DIM)
        s_buf[:, 0:reach] = lax.dot_general(
            q_buf[before:reach, part],
            k_buf[0:reach, part],
            (((1,), (1,)), ((), ())),
            preferred_element_type=jnp.float32,
        )
        tile = 16 if reach > 4 * rows else 32

        def softmax_tile(turn, carry):
            span = pl.ds(pl.multiple_of(turn * tile, tile), tile)
            row = lax.broadcasted_iota(jnp.int32, (tile, rows), 0) + turn * tile
            column = lax.broadcasted_iota(jnp.int32, (tile, rows), 1)
            last = jnp.where(column <= row, s_buf[span, before:reach], -1e30)
            highest = jnp.max(last, axis=1, keepdims=True)
            if index:
                early = s_buf[span, 0:before]
                highest = jnp.maximum(highest, jnp.max(early, axis=1, keepdims=True))
            top = highest * scale
            last = jnp.exp2(last * scale - top)
            total = jnp.sum(last, axis=1, keepdims=True)
            p_buf[span, before:reach] = last.astype(jnp.bfloat16)
            if index:
                early = jnp.exp2(early * scale - top)
                total += jnp.sum(early, axis=1, keepdims=True)
                p_buf[span, 0:before] = early.astype(jnp.bfloat16)
            l_buf[span, :] = jnp.broadcast_to(total, (tile, HEAD_DIM))
            return carry

        lax.fori_loop(0, rows // tile, softmax_tile, 0, unroll=2)
        update = dot32(p_buf[:, 0:reach], m_buf[0:reach, part])
        a_buf[before:reach, part] = (update / l_buf[...]).astype(jnp.bfloat16)

    wait_stream(3)
    wait_stream(4)

    def att_step(turn, carry):
        step = ordered(turn)
        for index in range(shards):
            @pl.when(partner(step) == index)
            def _():
                for head in range(heads):
                    attend(head, index)

        @pl.when(turn < shards)
        def _():
            att_send(step).start()

        return carry

    lax.fori_loop(1, shards + 1, att_step, 0)
    att_own().start()
    mixed_own().wait()
    att_own().wait()

    def out_arrived(slot, target, step):
        pltpu.make_async_remote_copy(
            src_ref=target,
            dst_ref=target,
            send_sem=out_send.at[slot, step],
            recv_sem=out_recv.at[slot, partner(step)],
            device_id={"ctx": partner(step)},
            device_id_type=MESH,
        ).wait_recv()

    def finish(step, carry):
        for stream in range(len(streams)):
            send(stream, step).wait_send()
        mixed_send(step).wait_send()
        att_send(step).wait_send()
        out_arrived(0, mixed_in.at[:, columns(partner(step))], step)
        out_arrived(1, att_in.at[:, columns(partner(step))], step)
        return carry

    lax.fori_loop(1, shards, finish, 0)


def by_heads(gate_input, value_input, filter_taps, skip_gain, queries, keys):
    shards = lax.axis_size("ctx")
    rows, channels = value_input.shape
    width = channels // shards
    length = shards * rows
    streams = 5
    in_place = pl.BlockSpec(memory_space=pl.ANY)
    landing = pltpu.VMEM((rows, channels), jnp.bfloat16)
    shape = jax.ShapeDtypeStruct((rows, channels), jnp.bfloat16)
    forward_hi, forward_lo, inverse_hi, inverse_lo = block_transforms(rows)
    results = pl.pallas_call(
        functools.partial(fused_kernel, shards),
        out_shape=(landing, landing),
        in_specs=[in_place] * 10,
        out_specs=(in_place, in_place),
        scratch_shapes=[
            pltpu.VMEM((rows, channels), jnp.float32),
            pltpu.VMEM((rows, channels), jnp.bfloat16),
            pltpu.VMEM((length, width), jnp.bfloat16),
            pltpu.VMEM((length, width), jnp.bfloat16),
            pltpu.VMEM((length, width), jnp.bfloat16),
            pltpu.VMEM((length, width), jnp.bfloat16),
            pltpu.VMEM((length, width), jnp.bfloat16),
            pltpu.VMEM((shards, 2 * rows, width), jnp.float32),
            pltpu.VMEM((shards, 2 * rows, width), jnp.float32),
            pltpu.VMEM((shards, 2 * rows, width), jnp.float32),
            pltpu.VMEM((length, width), jnp.bfloat16),
            pltpu.VMEM((length, width), jnp.bfloat16),
            pltpu.VMEM((rows, length), jnp.float32),
            pltpu.VMEM((rows, length), jnp.bfloat16),
            pltpu.VMEM((rows, HEAD_DIM), jnp.float32),
            pltpu.VMEM((2 * rows, 2 * rows), jnp.bfloat16),
            pltpu.VMEM((2 * rows, 2 * rows), jnp.bfloat16),
            pltpu.VMEM((rows, 2 * rows), jnp.bfloat16),
            pltpu.VMEM((rows, 2 * rows), jnp.bfloat16),
            pltpu.VMEM((1, channels), jnp.float32),
            pltpu.SemaphoreType.DMA((streams,)),
            pltpu.SemaphoreType.DMA((streams, shards)),
            pltpu.SemaphoreType.DMA((streams, shards)),
            pltpu.SemaphoreType.DMA((2, shards)),
            pltpu.SemaphoreType.DMA((2, shards)),
            pltpu.SemaphoreType.DMA((2,)),
            pltpu.SemaphoreType.DMA((5,)),
        ],
        compiler_params=pltpu.CompilerParams(
            collective_id=0, has_side_effects=True, vmem_limit_bytes=56 * 1024 * 1024
        ),
        name="conv_attention",
    )(
        forward_hi, forward_lo, inverse_hi, inverse_lo, skip_gain.reshape(1, channels),
        gate_input, value_input, filter_taps, queries, keys,
    )
    return pl.pallas_call(
        hand_over,
        out_shape=(shape, shape),
        in_specs=[in_place] * 2,
        out_specs=(in_place, in_place),
        scratch_shapes=[pltpu.SemaphoreType.DMA((2, HAND_OVERS))],
        compiler_params=pltpu.CompilerParams(vmem_limit_bytes=4 * 1024 * 1024),
        name="hand_over",
    )(*results)


HAND_OVERS = 4


def hand_over(first, second, first_out, second_out, sems):
    rows = first.shape[0] // HAND_OVERS
    copies = []
    for part in range(HAND_OVERS):
        span = pl.ds(part * rows, rows)
        for number, (source, target) in enumerate(((first, first_out), (second, second_out))):
            copies.append(pltpu.make_async_copy(source.at[span, :], target.at[span, :], sems.at[number, part]))
    for copy in copies:
        copy.start()
    for copy in copies:
        copy.wait()


def per_device(gate_input, value_input, filter_taps, skip_gain, queries, keys):
    shards = lax.axis_size("ctx")
    channels = value_input.shape[1]
    whole_heads = channels % (shards * HEAD_DIM) == 0
    run = by_heads if whole_heads else by_sequence
    return run(gate_input, value_input, filter_taps, skip_gain, queries, keys)


def solution(mesh):
    placed = (
        P("ctx", "tp"),
        P("ctx", "tp"),
        P("ctx", "tp"),
        P("tp"),
        P("ctx", "tp"),
        P("ctx", "tp"),
    )
    return jax.shard_map(
        per_device,
        mesh=mesh,
        in_specs=placed,
        out_specs=(P("ctx", "tp"), P("ctx", "tp")),
        check_vma=False,
    )
```

```python
import functools
import math

import jax
import jax.numpy as jnp
import numpy as np
from jax import lax
from jax.experimental import pallas as pl
from jax.experimental.pallas import tpu as pltpu
from jax.sharding import PartitionSpec as P

HEAD_DIM = 128


PRECISE = lax.Precision.HIGHEST
TWO_PI = 2.0 * math.pi


def as_sent(value):

    def short(part):
        return part.astype(jnp.bfloat16) if part.dtype == jnp.float32 else part

    return jax.tree.map(short, value)


def unit_roots(first_index, second_index, period, orient):
    product = first_index[:, None] * second_index[None, :] % period
    angles = TWO_PI / period * product.astype(jnp.float32)
    return (jnp.cos(angles), orient * jnp.sin(angles))


def first_section(signal, shards):
    cosine, sine_part = unit_roots(
        jnp.arange(2 * shards, dtype=jnp.int32),
        jnp.arange(shards, dtype=jnp.int32),
        2 * shards,
        -1.0,
    )
    real_part = jnp.einsum("kn,nmc->kmc", cosine, signal, precision=PRECISE)
    imag_part = jnp.einsum("kn,nmc->kmc", sine_part, signal, precision=PRECISE)
    return (real_part, imag_part)


def twist(real_part, imag_part, outer_index, inner_index, padded, orient):
    cosine, sine_part = unit_roots(outer_index, inner_index, padded, orient)
    cosine = cosine[:, :, None]
    sine_part = sine_part[:, :, None]
    return (real_part * cosine - imag_part * sine_part, real_part * sine_part + imag_part * cosine)


def contract(matrix, operand):
    return jnp.einsum("qn,knc->kqc", matrix, operand, precision=PRECISE)


def second_section(real_part, imag_part, orient):
    length = real_part.shape[1]
    indices = jnp.arange(length, dtype=jnp.int32)
    cosine, sine_part = unit_roots(indices, indices, length, orient)
    new_real = contract(cosine, real_part) - contract(sine_part, imag_part)
    new_imag = contract(sine_part, real_part) + contract(cosine, imag_part)
    return (new_real, new_imag)


def last_section(real_part, imag_part, shards, padded):
    cosine, sine_part = unit_roots(
        jnp.arange(shards, dtype=jnp.int32),
        jnp.arange(2 * shards, dtype=jnp.int32),
        2 * shards,
        1.0,
    )
    summed = jnp.einsum("nk,kmc->nmc", cosine, real_part, precision=PRECISE) - jnp.einsum(
        "nk,kmc->nmc", sine_part, imag_part, precision=PRECISE
    )
    return summed * (1.0 / padded)


def spectral_product(signal_spectrum, filter_spectrum):
    signal_real, signal_imag = signal_spectrum
    filter_real, filter_imag = filter_spectrum
    return (
        signal_real * filter_real - signal_imag * filter_imag,
        signal_real * filter_imag + signal_imag * filter_real,
    )


def by_sequence(gate_input, value_input, filter_taps, skip_gain, queries, keys):
    shards = lax.axis_size("ctx")
    my_index = lax.axis_index("ctx")
    tok_rows, channels = value_input.shape
    padded = 2 * shards * tok_rows
    signal = value_input.astype(jnp.float32)
    wide_index = jnp.arange(2 * shards, dtype=jnp.int32)
    slab_rows = tok_rows // shards
    moved_signal, moved_taps = (
        lax.all_to_all(
            signal.reshape(1, tok_rows, channels).astype(jnp.bfloat16),
            "ctx",
            split_axis=1,
            concat_axis=0,
            tiled=True,
        ).astype(jnp.float32),
        lax.all_to_all(
            filter_taps.reshape(1, tok_rows, channels).astype(jnp.bfloat16),
            "ctx",
            split_axis=1,
            concat_axis=0,
            tiled=True,
        ).astype(jnp.float32),
    )
    inner_index = my_index * slab_rows + jnp.arange(slab_rows, dtype=jnp.int32)

    def spread_front(block):
        real_part, imag_part = first_section(block, shards)
        real_part, imag_part = twist(real_part, imag_part, wide_index, inner_index, padded, -1.0)
        return jnp.stack([real_part, imag_part])

    turned_signal, turned_taps = (
        lax.all_to_all(
            as_sent(spread_front(moved_signal)), "ctx", split_axis=1, concat_axis=2, tiled=True
        ),
        lax.all_to_all(
            as_sent(spread_front(moved_taps)), "ctx", split_axis=1, concat_axis=2, tiled=True
        ),
    )
    signal_spectrum = second_section(turned_signal[0], turned_signal[1], -1.0)
    filter_spectrum = second_section(turned_taps[0], turned_taps[1], -1.0)
    real_part, imag_part = spectral_product(signal_spectrum, filter_spectrum)
    real_part, imag_part = second_section(real_part, imag_part, 1.0)
    outer_index = 2 * my_index + jnp.arange(2, dtype=jnp.int32)
    real_part, imag_part = twist(
        real_part, imag_part, outer_index, jnp.arange(tok_rows, dtype=jnp.int32), padded, 1.0
    )
    returned = lax.all_to_all(
        as_sent(jnp.stack([real_part, imag_part])), "ctx", split_axis=2, concat_axis=1, tiled=True
    )
    blocks = last_section(returned[0], returned[1], shards, padded)
    convolved = (
        lax.all_to_all(as_sent(blocks), "ctx", split_axis=0, concat_axis=1, tiled=True)
        .astype(blocks.dtype)
        .reshape(tok_rows, channels)
    )
    mixed = (gate_input.astype(jnp.float32) * (convolved + skip_gain[None, :] * signal)).astype(
        jnp.bfloat16
    )
    head_count = channels // HEAD_DIM
    scale_factor = 1.0 / math.sqrt(HEAD_DIM)
    query_heads = queries.reshape(tok_rows, head_count, HEAD_DIM)
    query_pos = my_index * tok_rows + jnp.arange(tok_rows, dtype=jnp.int32)
    running_max = jnp.full((head_count, tok_rows), -1e30, jnp.float32)
    key_block = lax.all_gather(keys, "ctx", axis=0, tiled=True)
    value_block = lax.all_gather(mixed, "ctx", axis=0, tiled=True)
    key_rows = key_block.shape[0]
    key_heads = key_block.reshape(key_rows, head_count, HEAD_DIM)
    value_heads = value_block.reshape(key_rows, head_count, HEAD_DIM)
    scores = (
        jnp.einsum("qhd,khd->hqk", query_heads, key_heads, preferred_element_type=jnp.float32)
        * scale_factor
    )
    key_pos = jnp.arange(key_rows, dtype=jnp.int32)
    allowed = (key_pos[None, :] <= query_pos[:, None])[None]
    masked = jnp.where(allowed, scores, -1e30)
    newest = jnp.maximum(running_max, jnp.max(masked, axis=2))
    weights = jnp.where(allowed, jnp.exp(masked - newest[:, :, None]), 0.0)
    total_weight = jnp.sum(weights, axis=2)
    update = jnp.einsum(
        "hqk,khd->hqd",
        weights.astype(jnp.bfloat16),
        value_heads,
        preferred_element_type=jnp.float32,
    )
    accumulated = update
    running_max, total_weight, accumulated = (newest, total_weight, accumulated)
    attended = (
        (accumulated / total_weight[:, :, None])
        .transpose(1, 0, 2)
        .reshape(tok_rows, channels)
        .astype(jnp.bfloat16)
    )
    return (mixed, attended)


MESH = pl.DeviceIdType.MESH
LANES = 128
SUBLANES = 8


def split_bf16(matrix):
    high = matrix.astype(jnp.bfloat16)
    low = (matrix - high.astype(np.float64)).astype(jnp.bfloat16)
    return high, low


def block_transforms(rows):
    lags = np.arange(-rows, rows, dtype=np.int64)
    turns = (2 * np.arange(rows, dtype=np.int64)[:, None] + 1) * lags[None, :] % (4 * rows)
    angles = 2.0 * np.pi / (4 * rows) * turns
    forward = np.concatenate([np.cos(angles), -np.sin(angles)], axis=0)
    inverse = forward[:, rows:].T / rows
    return split_bf16(forward) + split_bf16(inverse)


def dot32(left, right):
    return jnp.dot(left, right, preferred_element_type=jnp.float32)


def fused_kernel(
    shards, fwd_hi_in, fwd_lo_in, inv_hi_in, inv_lo_in, skip_in, gate, value, taps, queries, keys,
    mixed_in, att_in,
    taps_wide, taps_sent, v_buf, t_buf, g_buf, k_buf, q_buf, v_spec, h_spec, z_spec, m_buf, a_buf,
    s_buf, p_buf, l_buf, fwd_hi, fwd_lo, inv_hi, inv_lo, skip,
    own_sem, in_send, in_recv, out_send, out_recv, own_out, stage_sem,
):
    me = lax.axis_index("ctx")
    rows = value.shape[0]
    width = v_buf.shape[1]
    heads = width // HEAD_DIM

    def partner(step):
        if shards % 4:
            return lax.rem(me + step, shards)
        outer = shards // 4
        core = me % 2
        turn = step // 2
        along_x = (1 - core) * (turn % 2) + core * (turn // outer)
        along_y = (1 - core) * (turn // 2) + core * (turn % outer)
        new_core = (core + step) % 2
        new_x = (me // 2 + along_x) % 2
        new_y = (me // 4 + along_y) % outer
        return (new_y * 2 + new_x) * 2 + new_core

    def ordered(turn):
        return turn % (shards - 1) + 1 + (turn // shards) * (shards - 2)

    def block(index):
        return pl.ds(pl.multiple_of(index * rows, rows), rows)

    def columns(index):
        return pl.ds(pl.multiple_of(index * width, LANES), width)

    barrier = pltpu.get_barrier_semaphore()

    def greet(step, carry):
        pl.semaphore_signal(barrier, inc=1, device_id={"ctx": partner(step)}, device_id_type=MESH)
        return carry

    lax.fori_loop(1, shards, greet, 0)

    wide_copy = pltpu.make_async_copy(taps, taps_wide, own_out.at[0])
    wide_copy.start()
    staged = [
        pltpu.make_async_copy(source, target, stage_sem.at[number])
        for number, (source, target) in enumerate(
            (
                (fwd_hi_in, fwd_hi), (fwd_lo_in, fwd_lo), (skip_in, skip),
                (inv_hi_in, inv_hi), (inv_lo_in, inv_lo),
            )
        )
    ]
    streams = [(value, v_buf), (taps_sent, t_buf), (gate, g_buf), (keys, k_buf), (queries, q_buf)]

    def own_copy(stream):
        source, target = streams[stream]
        return pltpu.make_async_copy(
            source.at[:, columns(me)], target.at[block(me), :], own_sem.at[stream]
        )

    def send(stream, step):
        source, target = streams[stream]
        peer = partner(step)
        return pltpu.make_async_remote_copy(
            src_ref=source.at[:, columns(peer)],
            dst_ref=target.at[block(me), :],
            send_sem=in_send.at[stream, step],
            recv_sem=in_recv.at[stream, me],
            device_id={"ctx": peer},
            device_id_type=MESH,
        )

    def start_stream(stream):
        def one(turn, carry):
            send(stream, ordered(turn)).start()
            return carry

        own_copy(stream).start()
        lax.fori_loop(1, shards, one, 0)

    def arrived(stream, step):
        target = streams[stream][1].at[block(partner(step)), :]
        pltpu.make_async_remote_copy(
            src_ref=target,
            dst_ref=target,
            send_sem=in_send.at[stream, step],
            recv_sem=in_recv.at[stream, partner(step)],
            device_id={"ctx": partner(step)},
            device_id_type=MESH,
        ).wait_recv()

    def wait_stream(stream):
        def one(step, carry):
            arrived(stream, step)
            return carry

        own_copy(stream).wait()
        lax.fori_loop(1, shards, one, 0)

    pl.semaphore_wait(barrier, shards - 1)
    start_stream(0)
    for copy in staged:
        copy.start()
    wide_copy.wait()
    taps_sent[...] = taps_wide[...].astype(jnp.bfloat16)
    start_stream(1)
    start_stream(2)

    def spectrum(index):
        signal = v_buf[block(index), :]
        v_spec[index] = dot32(fwd_hi[:, rows:], signal) + dot32(fwd_lo[:, rows:], signal)

    for copy in staged:
        copy.wait()
    own_copy(0).wait()
    spectrum(me)

    def signal_step(turn, carry):
        step = ordered(turn)
        arrived(0, step)
        spectrum(partner(step))
        return carry

    lax.fori_loop(1, shards, signal_step, 0)

    wait_stream(1)
    start_stream(3)
    start_stream(4)
    first = t_buf[0:rows, :]
    h_spec[0] = dot32(fwd_hi[:, rows:], first) + dot32(fwd_lo[:, rows:], first)

    def taps_step(index, carry):
        window = t_buf[pl.ds(pl.multiple_of((index - 1) * rows, rows), 2 * rows), :]
        h_spec[index] = dot32(fwd_hi[...], window) + dot32(fwd_lo[...], window)
        return carry

    lax.fori_loop(1, shards, taps_step, 0)

    def product_step(chunk, carry):
        real = pl.ds(pl.multiple_of(chunk * SUBLANES, SUBLANES), SUBLANES)
        imag = pl.ds(pl.multiple_of(rows + chunk * SUBLANES, SUBLANES), SUBLANES)
        for lane in range(0, width, LANES):
            part = slice(lane, lane + LANES)
            v_real = [v_spec[i, real, part] for i in range(shards)]
            v_imag = [v_spec[i, imag, part] for i in range(shards)]
            h_real = [h_spec[i, real, part] for i in range(shards)]
            h_imag = [h_spec[i, imag, part] for i in range(shards)]
            for out in range(shards):
                total_real = v_real[0] * h_real[out] - v_imag[0] * h_imag[out]
                total_imag = v_real[0] * h_imag[out] + v_imag[0] * h_real[out]
                for i in range(1, out + 1):
                    total_real += v_real[i] * h_real[out - i] - v_imag[i] * h_imag[out - i]
                    total_imag += v_real[i] * h_imag[out - i] + v_imag[i] * h_real[out - i]
                z_spec[out, real, part] = total_real
                z_spec[out, imag, part] = total_imag
        return carry

    lax.fori_loop(0, rows // SUBLANES, product_step, 0)

    wait_stream(2)
    gain = skip[:, columns(me)]

    def mix(index):
        summed = z_spec[index]
        high = summed.astype(jnp.bfloat16)
        low = (summed - high.astype(jnp.float32)).astype(jnp.bfloat16)
        convolved = dot32(inv_hi[...], high) + dot32(inv_lo[...], high) + dot32(inv_hi[...], low)
        signal = v_buf[block(index), :].astype(jnp.float32)
        opened = g_buf[block(index), :].astype(jnp.float32)
        m_buf[block(index), :] = (opened * (convolved + gain * signal)).astype(jnp.bfloat16)

    def mixed_send(step):
        peer = partner(step)
        return pltpu.make_async_remote_copy(
            src_ref=m_buf.at[block(peer), :],
            dst_ref=mixed_in.at[:, columns(me)],
            send_sem=out_send.at[0, step],
            recv_sem=out_recv.at[0, me],
            device_id={"ctx": peer},
            device_id_type=MESH,
        )

    def mixed_own():
        return pltpu.make_async_copy(m_buf.at[block(me), :], mixed_in.at[:, columns(me)], own_out.at[0])

    def mix_step(turn, carry):
        step = ordered(turn)
        mix(partner(step))
        return carry

    lax.fori_loop(1, shards, mix_step, 0)
    mix(me)
    mixed_own().start()

    def left(step, carry):
        send(3, step).wait_send()
        send(4, step).wait_send()
        return carry

    def return_mixed(turn, carry):
        mixed_send(ordered(turn)).start()
        return carry

    lax.fori_loop(1, shards, left, 0)
    lax.fori_loop(1, shards, return_mixed, 0)

    scale = math.log2(math.e) / math.sqrt(HEAD_DIM)

    def att_send(step):
        peer = partner(step)
        return pltpu.make_async_remote_copy(
            src_ref=a_buf.at[block(peer), :],
            dst_ref=att_in.at[:, columns(me)],
            send_sem=out_send.at[1, step],
            recv_sem=out_recv.at[1, me],
            device_id={"ctx": peer},
            device_id_type=MESH,
        )

    def att_own():
        return pltpu.make_async_copy(a_buf.at[block(me), :], att_in.at[:, columns(me)], own_out.at[1])

    def attend(head, index):
        reach = (index + 1) * rows
        before = index * rows
        part = slice(head * HEAD_DIM, (head + 1) * HEAD_DIM)
        s_buf[:, 0:reach] = lax.dot_general(
            q_buf[before:reach, part],
            k_buf[0:reach, part],
            (((1,), (1,)), ((), ())),
            preferred_element_type=jnp.float32,
        )
        tile = 16 if reach > 4 * rows else 32

        def softmax_tile(turn, carry):
            span = pl.ds(pl.multiple_of(turn * tile, tile), tile)
            row = lax.broadcasted_iota(jnp.int32, (tile, rows), 0) + turn * tile
            column = lax.broadcasted_iota(jnp.int32, (tile, rows), 1)
            last = jnp.where(column <= row, s_buf[span, before:reach], -1e30)
            highest = jnp.max(last, axis=1, keepdims=True)
            if index:
                early = s_buf[span, 0:before]
                highest = jnp.maximum(highest, jnp.max(early, axis=1, keepdims=True))
            top = highest * scale
            last = jnp.exp2(last * scale - top)
            total = jnp.sum(last, axis=1, keepdims=True)
            p_buf[span, before:reach] = last.astype(jnp.bfloat16)
            if index:
                early = jnp.exp2(early * scale - top)
                total += jnp.sum(early, axis=1, keepdims=True)
                p_buf[span, 0:before] = early.astype(jnp.bfloat16)
            l_buf[span, :] = jnp.broadcast_to(total, (tile, HEAD_DIM))
            return carry

        lax.fori_loop(0, rows // tile, softmax_tile, 0, unroll=2)
        update = dot32(p_buf[:, 0:reach], m_buf[0:reach, part])
        a_buf[before:reach, part] = (update / l_buf[...]).astype(jnp.bfloat16)

    wait_stream(3)
    wait_stream(4)

    def att_step(turn, carry):
        step = ordered(turn)
        for index in range(shards):
            @pl.when(partner(step) == index)
            def _():
                for head in range(heads):
                    attend(head, index)

        @pl.when(turn < shards)
        def _():
            att_send(step).start()

        return carry

    lax.fori_loop(1, shards + 1, att_step, 0)
    att_own().start()
    mixed_own().wait()
    att_own().wait()

    def out_arrived(slot, target, step):
        pltpu.make_async_remote_copy(
            src_ref=target,
            dst_ref=target,
            send_sem=out_send.at[slot, step],
            recv_sem=out_recv.at[slot, partner(step)],
            device_id={"ctx": partner(step)},
            device_id_type=MESH,
        ).wait_recv()

    def finish(step, carry):
        for stream in range(3):
            send(stream, step).wait_send()
        mixed_send(step).wait_send()
        att_send(step).wait_send()
        out_arrived(0, mixed_in.at[:, columns(partner(step))], step)
        out_arrived(1, att_in.at[:, columns(partner(step))], step)
        return carry

    lax.fori_loop(1, shards, finish, 0)


def by_heads(gate_input, value_input, filter_taps, skip_gain, queries, keys):
    shards = lax.axis_size("ctx")
    rows, channels = value_input.shape
    width = channels // shards
    length = shards * rows
    streams = 5
    in_place = pl.BlockSpec(memory_space=pl.ANY)
    landing = pltpu.VMEM((rows, channels), jnp.bfloat16)
    shape = jax.ShapeDtypeStruct((rows, channels), jnp.bfloat16)
    forward_hi, forward_lo, inverse_hi, inverse_lo = block_transforms(rows)
    results = pl.pallas_call(
        functools.partial(fused_kernel, shards),
        out_shape=(landing, landing),
        in_specs=[in_place] * 10,
        out_specs=(in_place, in_place),
        scratch_shapes=[
            pltpu.VMEM((rows, channels), jnp.float32),
            pltpu.VMEM((rows, channels), jnp.bfloat16),
            pltpu.VMEM((length, width), jnp.bfloat16),
            pltpu.VMEM((length, width), jnp.bfloat16),
            pltpu.VMEM((length, width), jnp.bfloat16),
            pltpu.VMEM((length, width), jnp.bfloat16),
            pltpu.VMEM((length, width), jnp.bfloat16),
            pltpu.VMEM((shards, 2 * rows, width), jnp.float32),
            pltpu.VMEM((shards, 2 * rows, width), jnp.float32),
            pltpu.VMEM((shards, 2 * rows, width), jnp.float32),
            pltpu.VMEM((length, width), jnp.bfloat16),
            pltpu.VMEM((length, width), jnp.bfloat16),
            pltpu.VMEM((rows, length), jnp.float32),
            pltpu.VMEM((rows, length), jnp.bfloat16),
            pltpu.VMEM((rows, HEAD_DIM), jnp.float32),
            pltpu.VMEM((2 * rows, 2 * rows), jnp.bfloat16),
            pltpu.VMEM((2 * rows, 2 * rows), jnp.bfloat16),
            pltpu.VMEM((rows, 2 * rows), jnp.bfloat16),
            pltpu.VMEM((rows, 2 * rows), jnp.bfloat16),
            pltpu.VMEM((1, channels), jnp.float32),
            pltpu.SemaphoreType.DMA((streams,)),
            pltpu.SemaphoreType.DMA((streams, shards)),
            pltpu.SemaphoreType.DMA((streams, shards)),
            pltpu.SemaphoreType.DMA((2, shards)),
            pltpu.SemaphoreType.DMA((2, shards)),
            pltpu.SemaphoreType.DMA((2,)),
            pltpu.SemaphoreType.DMA((5,)),
        ],
        compiler_params=pltpu.CompilerParams(
            collective_id=0, has_side_effects=True, vmem_limit_bytes=56 * 1024 * 1024
        ),
        name="conv_attention",
    )(
        forward_hi, forward_lo, inverse_hi, inverse_lo, skip_gain.reshape(1, channels),
        gate_input, value_input, filter_taps, queries, keys,
    )
    return pl.pallas_call(
        hand_over,
        out_shape=(shape, shape),
        in_specs=[in_place] * 2,
        out_specs=(in_place, in_place),
        scratch_shapes=[pltpu.SemaphoreType.DMA((2, HAND_OVERS))],
        compiler_params=pltpu.CompilerParams(vmem_limit_bytes=4 * 1024 * 1024),
        name="hand_over",
    )(*results)


HAND_OVERS = 4


def hand_over(first, second, first_out, second_out, sems):
    rows = first.shape[0] // HAND_OVERS
    copies = []
    for part in range(HAND_OVERS):
        span = pl.ds(part * rows, rows)
        for number, (source, target) in enumerate(((first, first_out), (second, second_out))):
            copies.append(pltpu.make_async_copy(source.at[span, :], target.at[span, :], sems.at[number, part]))
    for copy in copies:
        copy.start()
    for copy in copies:
        copy.wait()


def per_device(gate_input, value_input, filter_taps, skip_gain, queries, keys):
    shards = lax.axis_size("ctx")
    channels = value_input.shape[1]
    whole_heads = channels % (shards * HEAD_DIM) == 0
    run = by_heads if whole_heads else by_sequence
    return run(gate_input, value_input, filter_taps, skip_gain, queries, keys)


def solution(mesh):
    placed = (
        P("ctx", "tp"),
        P("ctx", "tp"),
        P("ctx", "tp"),
        P("tp"),
        P("ctx", "tp"),
        P("ctx", "tp"),
    )
    return jax.shard_map(
        per_device,
        mesh=mesh,
        in_specs=placed,
        out_specs=(P("ctx", "tp"), P("ctx", "tp")),
        check_vma=False,
    )
```

```python
import functools
import math

import jax
import jax.numpy as jnp
import numpy as np
from jax import lax
from jax.experimental import pallas as pl
from jax.experimental.pallas import tpu as pltpu
from jax.sharding import PartitionSpec as P

HEAD_DIM = 128


PRECISE = lax.Precision.HIGHEST
TWO_PI = 2.0 * math.pi


def as_sent(value):

    def short(part):
        return part.astype(jnp.bfloat16) if part.dtype == jnp.float32 else part

    return jax.tree.map(short, value)


def unit_roots(first_index, second_index, period, orient):
    product = first_index[:, None] * second_index[None, :] % period
    angles = TWO_PI / period * product.astype(jnp.float32)
    return (jnp.cos(angles), orient * jnp.sin(angles))


def first_section(signal, shards):
    cosine, sine_part = unit_roots(
        jnp.arange(2 * shards, dtype=jnp.int32),
        jnp.arange(shards, dtype=jnp.int32),
        2 * shards,
        -1.0,
    )
    real_part = jnp.einsum("kn,nmc->kmc", cosine, signal, precision=PRECISE)
    imag_part = jnp.einsum("kn,nmc->kmc", sine_part, signal, precision=PRECISE)
    return (real_part, imag_part)


def twist(real_part, imag_part, outer_index, inner_index, padded, orient):
    cosine, sine_part = unit_roots(outer_index, inner_index, padded, orient)
    cosine = cosine[:, :, None]
    sine_part = sine_part[:, :, None]
    return (real_part * cosine - imag_part * sine_part, real_part * sine_part + imag_part * cosine)


def contract(matrix, operand):
    return jnp.einsum("qn,knc->kqc", matrix, operand, precision=PRECISE)


def second_section(real_part, imag_part, orient):
    length = real_part.shape[1]
    indices = jnp.arange(length, dtype=jnp.int32)
    cosine, sine_part = unit_roots(indices, indices, length, orient)
    new_real = contract(cosine, real_part) - contract(sine_part, imag_part)
    new_imag = contract(sine_part, real_part) + contract(cosine, imag_part)
    return (new_real, new_imag)


def last_section(real_part, imag_part, shards, padded):
    cosine, sine_part = unit_roots(
        jnp.arange(shards, dtype=jnp.int32),
        jnp.arange(2 * shards, dtype=jnp.int32),
        2 * shards,
        1.0,
    )
    summed = jnp.einsum("nk,kmc->nmc", cosine, real_part, precision=PRECISE) - jnp.einsum(
        "nk,kmc->nmc", sine_part, imag_part, precision=PRECISE
    )
    return summed * (1.0 / padded)


def spectral_product(signal_spectrum, filter_spectrum):
    signal_real, signal_imag = signal_spectrum
    filter_real, filter_imag = filter_spectrum
    return (
        signal_real * filter_real - signal_imag * filter_imag,
        signal_real * filter_imag + signal_imag * filter_real,
    )


def by_sequence(gate_input, value_input, filter_taps, skip_gain, queries, keys):
    shards = lax.axis_size("ctx")
    my_index = lax.axis_index("ctx")
    tok_rows, channels = value_input.shape
    padded = 2 * shards * tok_rows
    signal = value_input.astype(jnp.float32)
    wide_index = jnp.arange(2 * shards, dtype=jnp.int32)
    slab_rows = tok_rows // shards
    moved_signal, moved_taps = (
        lax.all_to_all(
            signal.reshape(1, tok_rows, channels).astype(jnp.bfloat16),
            "ctx",
            split_axis=1,
            concat_axis=0,
            tiled=True,
        ).astype(jnp.float32),
        lax.all_to_all(
            filter_taps.reshape(1, tok_rows, channels).astype(jnp.bfloat16),
            "ctx",
            split_axis=1,
            concat_axis=0,
            tiled=True,
        ).astype(jnp.float32),
    )
    inner_index = my_index * slab_rows + jnp.arange(slab_rows, dtype=jnp.int32)

    def spread_front(block):
        real_part, imag_part = first_section(block, shards)
        real_part, imag_part = twist(real_part, imag_part, wide_index, inner_index, padded, -1.0)
        return jnp.stack([real_part, imag_part])

    turned_signal, turned_taps = (
        lax.all_to_all(
            as_sent(spread_front(moved_signal)), "ctx", split_axis=1, concat_axis=2, tiled=True
        ),
        lax.all_to_all(
            as_sent(spread_front(moved_taps)), "ctx", split_axis=1, concat_axis=2, tiled=True
        ),
    )
    signal_spectrum = second_section(turned_signal[0], turned_signal[1], -1.0)
    filter_spectrum = second_section(turned_taps[0], turned_taps[1], -1.0)
    real_part, imag_part = spectral_product(signal_spectrum, filter_spectrum)
    real_part, imag_part = second_section(real_part, imag_part, 1.0)
    outer_index = 2 * my_index + jnp.arange(2, dtype=jnp.int32)
    real_part, imag_part = twist(
        real_part, imag_part, outer_index, jnp.arange(tok_rows, dtype=jnp.int32), padded, 1.0
    )
    returned = lax.all_to_all(
        as_sent(jnp.stack([real_part, imag_part])), "ctx", split_axis=2, concat_axis=1, tiled=True
    )
    blocks = last_section(returned[0], returned[1], shards, padded)
    convolved = (
        lax.all_to_all(as_sent(blocks), "ctx", split_axis=0, concat_axis=1, tiled=True)
        .astype(blocks.dtype)
        .reshape(tok_rows, channels)
    )
    mixed = (gate_input.astype(jnp.float32) * (convolved + skip_gain[None, :] * signal)).astype(
        jnp.bfloat16
    )
    head_count = channels // HEAD_DIM
    scale_factor = 1.0 / math.sqrt(HEAD_DIM)
    query_heads = queries.reshape(tok_rows, head_count, HEAD_DIM)
    query_pos = my_index * tok_rows + jnp.arange(tok_rows, dtype=jnp.int32)
    running_max = jnp.full((head_count, tok_rows), -1e30, jnp.float32)
    key_block = lax.all_gather(keys, "ctx", axis=0, tiled=True)
    value_block = lax.all_gather(mixed, "ctx", axis=0, tiled=True)
    key_rows = key_block.shape[0]
    key_heads = key_block.reshape(key_rows, head_count, HEAD_DIM)
    value_heads = value_block.reshape(key_rows, head_count, HEAD_DIM)
    scores = (
        jnp.einsum("qhd,khd->hqk", query_heads, key_heads, preferred_element_type=jnp.float32)
        * scale_factor
    )
    key_pos = jnp.arange(key_rows, dtype=jnp.int32)
    allowed = (key_pos[None, :] <= query_pos[:, None])[None]
    masked = jnp.where(allowed, scores, -1e30)
    newest = jnp.maximum(running_max, jnp.max(masked, axis=2))
    weights = jnp.where(allowed, jnp.exp(masked - newest[:, :, None]), 0.0)
    total_weight = jnp.sum(weights, axis=2)
    update = jnp.einsum(
        "hqk,khd->hqd",
        weights.astype(jnp.bfloat16),
        value_heads,
        preferred_element_type=jnp.float32,
    )
    accumulated = update
    running_max, total_weight, accumulated = (newest, total_weight, accumulated)
    attended = (
        (accumulated / total_weight[:, :, None])
        .transpose(1, 0, 2)
        .reshape(tok_rows, channels)
        .astype(jnp.bfloat16)
    )
    return (mixed, attended)


MESH = pl.DeviceIdType.MESH
LANES = 128
SUBLANES = 8


def split_bf16(matrix):
    high = matrix.astype(jnp.bfloat16)
    low = (matrix - high.astype(np.float64)).astype(jnp.bfloat16)
    return high, low


def block_transforms(rows):
    lags = np.arange(-rows, rows, dtype=np.int64)
    turns = (2 * np.arange(rows, dtype=np.int64)[:, None] + 1) * lags[None, :] % (4 * rows)
    angles = 2.0 * np.pi / (4 * rows) * turns
    forward = np.concatenate([np.cos(angles), -np.sin(angles)], axis=0)
    inverse = forward[:, rows:].T / rows
    return split_bf16(forward) + split_bf16(inverse)


def dot32(left, right):
    return jnp.dot(left, right, preferred_element_type=jnp.float32)


def fused_kernel(
    shards, fwd_hi_in, fwd_lo_in, inv_hi_in, inv_lo_in, skip_in, gate, value, taps, queries, keys,
    mixed_in, att_in,
    taps_wide, taps_sent, v_buf, t_buf, g_buf, k_buf, q_buf, v_spec, h_spec, z_spec, m_buf, a_buf,
    s_buf, p_buf, l_buf, fwd_hi, fwd_lo, inv_hi, inv_lo, skip,
    own_sem, in_send, in_recv, out_send, out_recv, own_out, stage_sem,
):
    me = lax.axis_index("ctx")
    rows = value.shape[0]
    width = v_buf.shape[1]
    heads = width // HEAD_DIM

    def partner(step):
        if shards % 4:
            return lax.rem(me + step, shards)
        outer = shards // 4
        core = me % 2
        turn = step // 2
        along_x = (1 - core) * (turn % 2) + core * (turn // outer)
        along_y = (1 - core) * (turn // 2) + core * (turn % outer)
        new_core = (core + step) % 2
        new_x = (me // 2 + along_x) % 2
        new_y = (me // 4 + along_y) % outer
        return (new_y * 2 + new_x) * 2 + new_core

    def ordered(turn):
        return turn % (shards - 1) + 1 + (turn // shards) * (shards - 2)

    def block(index):
        return pl.ds(pl.multiple_of(index * rows, rows), rows)

    def columns(index):
        return pl.ds(pl.multiple_of(index * width, LANES), width)

    barrier = pltpu.get_barrier_semaphore()

    def greet(step, carry):
        pl.semaphore_signal(barrier, inc=1, device_id={"ctx": partner(step)}, device_id_type=MESH)
        return carry

    lax.fori_loop(1, shards, greet, 0)

    wide_copy = pltpu.make_async_copy(taps, taps_wide, own_out.at[0])
    wide_copy.start()
    staged = [
        pltpu.make_async_copy(source, target, stage_sem.at[number])
        for number, (source, target) in enumerate(
            (
                (fwd_hi_in, fwd_hi), (fwd_lo_in, fwd_lo), (skip_in, skip),
                (inv_hi_in, inv_hi), (inv_lo_in, inv_lo),
            )
        )
    ]
    streams = [(value, v_buf), (taps_sent, t_buf), (gate, g_buf), (keys, k_buf), (queries, q_buf)]

    def own_copy(stream):
        source, target = streams[stream]
        return pltpu.make_async_copy(
            source.at[:, columns(me)], target.at[block(me), :], own_sem.at[stream]
        )

    def send(stream, step):
        source, target = streams[stream]
        peer = partner(step)
        return pltpu.make_async_remote_copy(
            src_ref=source.at[:, columns(peer)],
            dst_ref=target.at[block(me), :],
            send_sem=in_send.at[stream, step],
            recv_sem=in_recv.at[stream, me],
            device_id={"ctx": peer},
            device_id_type=MESH,
        )

    def start_stream(stream):
        def one(turn, carry):
            send(stream, ordered(turn)).start()
            return carry

        own_copy(stream).start()
        lax.fori_loop(1, shards, one, 0)

    def arrived(stream, step):
        target = streams[stream][1].at[block(partner(step)), :]
        pltpu.make_async_remote_copy(
            src_ref=target,
            dst_ref=target,
            send_sem=in_send.at[stream, step],
            recv_sem=in_recv.at[stream, partner(step)],
            device_id={"ctx": partner(step)},
            device_id_type=MESH,
        ).wait_recv()

    def wait_stream(stream):
        def one(step, carry):
            arrived(stream, step)
            return carry

        own_copy(stream).wait()
        lax.fori_loop(1, shards, one, 0)

    pl.semaphore_wait(barrier, shards - 1)
    start_stream(0)
    for copy in staged:
        copy.start()
    wide_copy.wait()
    taps_sent[...] = taps_wide[...].astype(jnp.bfloat16)
    start_stream(1)
    start_stream(2)

    def spectrum(index):
        signal = v_buf[block(index), :]
        v_spec[index] = dot32(fwd_hi[:, rows:], signal) + dot32(fwd_lo[:, rows:], signal)

    for copy in staged:
        copy.wait()
    own_copy(0).wait()
    spectrum(me)

    def signal_step(turn, carry):
        step = ordered(turn)
        arrived(0, step)
        spectrum(partner(step))
        return carry

    lax.fori_loop(1, shards, signal_step, 0)

    wait_stream(1)
    start_stream(3)
    start_stream(4)
    first = t_buf[0:rows, :]
    h_spec[0] = dot32(fwd_hi[:, rows:], first) + dot32(fwd_lo[:, rows:], first)

    def taps_step(index, carry):
        window = t_buf[pl.ds(pl.multiple_of((index - 1) * rows, rows), 2 * rows), :]
        h_spec[index] = dot32(fwd_hi[...], window) + dot32(fwd_lo[...], window)
        return carry

    lax.fori_loop(1, shards, taps_step, 0)

    def product_step(chunk, carry):
        real = pl.ds(pl.multiple_of(chunk * SUBLANES, SUBLANES), SUBLANES)
        imag = pl.ds(pl.multiple_of(rows + chunk * SUBLANES, SUBLANES), SUBLANES)
        for lane in range(0, width, LANES):
            part = slice(lane, lane + LANES)
            v_real = [v_spec[i, real, part] for i in range(shards)]
            v_imag = [v_spec[i, imag, part] for i in range(shards)]
            h_real = [h_spec[i, real, part] for i in range(shards)]
            h_imag = [h_spec[i, imag, part] for i in range(shards)]
            for out in range(shards):
                total_real = v_real[0] * h_real[out] - v_imag[0] * h_imag[out]
                total_imag = v_real[0] * h_imag[out] + v_imag[0] * h_real[out]
                for i in range(1, out + 1):
                    total_real += v_real[i] * h_real[out - i] - v_imag[i] * h_imag[out - i]
                    total_imag += v_real[i] * h_imag[out - i] + v_imag[i] * h_real[out - i]
                z_spec[out, real, part] = total_real
                z_spec[out, imag, part] = total_imag
        return carry

    lax.fori_loop(0, rows // SUBLANES, product_step, 0)

    wait_stream(2)
    gain = skip[:, columns(me)]

    def mix(index):
        summed = z_spec[index]
        high = summed.astype(jnp.bfloat16)
        low = (summed - high.astype(jnp.float32)).astype(jnp.bfloat16)
        convolved = dot32(inv_hi[...], high) + dot32(inv_lo[...], high) + dot32(inv_hi[...], low)
        signal = v_buf[block(index), :].astype(jnp.float32)
        opened = g_buf[block(index), :].astype(jnp.float32)
        m_buf[block(index), :] = (opened * (convolved + gain * signal)).astype(jnp.bfloat16)

    def mixed_send(step):
        peer = partner(step)
        return pltpu.make_async_remote_copy(
            src_ref=m_buf.at[block(peer), :],
            dst_ref=mixed_in.at[:, columns(me)],
            send_sem=out_send.at[0, step],
            recv_sem=out_recv.at[0, me],
            device_id={"ctx": peer},
            device_id_type=MESH,
        )

    def mixed_own():
        return pltpu.make_async_copy(m_buf.at[block(me), :], mixed_in.at[:, columns(me)], own_out.at[0])

    def mix_step(turn, carry):
        step = ordered(turn)
        mix(partner(step))
        return carry

    lax.fori_loop(1, shards, mix_step, 0)
    mix(me)
    mixed_own().start()

    def left(step, carry):
        send(3, step).wait_send()
        send(4, step).wait_send()
        return carry

    def return_mixed(turn, carry):
        mixed_send(ordered(turn)).start()
        return carry

    lax.fori_loop(1, shards, left, 0)
    lax.fori_loop(1, shards, return_mixed, 0)

    scale = math.log2(math.e) / math.sqrt(HEAD_DIM)

    def att_send(step):
        peer = partner(step)
        return pltpu.make_async_remote_copy(
            src_ref=a_buf.at[block(peer), :],
            dst_ref=att_in.at[:, columns(me)],
            send_sem=out_send.at[1, step],
            recv_sem=out_recv.at[1, me],
            device_id={"ctx": peer},
            device_id_type=MESH,
        )

    def att_own():
        return pltpu.make_async_copy(a_buf.at[block(me), :], att_in.at[:, columns(me)], own_out.at[1])

    def attend(head, index):
        reach = (index + 1) * rows
        before = index * rows
        part = slice(head * HEAD_DIM, (head + 1) * HEAD_DIM)
        s_buf[:, 0:reach] = lax.dot_general(
            q_buf[before:reach, part],
            k_buf[0:reach, part],
            (((1,), (1,)), ((), ())),
            preferred_element_type=jnp.float32,
        )
        row = lax.broadcasted_iota(jnp.int32, (rows, rows), 0)
        column = lax.broadcasted_iota(jnp.int32, (rows, rows), 1)
        s_buf[:, before:reach] = jnp.where(column <= row, s_buf[:, before:reach], -1e30)
        highest = s_buf[:, 0:LANES]
        for lane in range(LANES, reach, LANES):
            highest = jnp.maximum(highest, s_buf[:, lane : lane + LANES])
        l_buf[...] = jnp.broadcast_to(jnp.max(highest, axis=1, keepdims=True) * scale, (rows, LANES))
        tile = rows // 2
        for start in range(0, rows, tile):
            span = slice(start, start + tile)
            top = l_buf[span, :]
            total = jnp.zeros((tile, LANES), jnp.float32)
            for lane in range(0, reach, LANES):
                weights = jnp.exp2(s_buf[span, lane : lane + LANES] * scale - top)
                total += weights
                p_buf[span, lane : lane + LANES] = weights.astype(jnp.bfloat16)
            l_buf[span, :] = jnp.broadcast_to(jnp.sum(total, axis=1, keepdims=True), (tile, LANES))
        update = dot32(p_buf[:, 0:reach], m_buf[0:reach, part])
        a_buf[before:reach, part] = (update / l_buf[...]).astype(jnp.bfloat16)

    wait_stream(3)
    wait_stream(4)

    def att_step(turn, carry):
        step = ordered(turn)
        for index in range(shards):
            @pl.when(partner(step) == index)
            def _():
                for head in range(heads):
                    attend(head, index)

        @pl.when(turn < shards)
        def _():
            att_send(step).start()

        return carry

    lax.fori_loop(1, shards + 1, att_step, 0)
    att_own().start()
    mixed_own().wait()
    att_own().wait()

    def out_arrived(slot, target, step):
        pltpu.make_async_remote_copy(
            src_ref=target,
            dst_ref=target,
            send_sem=out_send.at[slot, step],
            recv_sem=out_recv.at[slot, partner(step)],
            device_id={"ctx": partner(step)},
            device_id_type=MESH,
        ).wait_recv()

    def finish(step, carry):
        for stream in range(3):
            send(stream, step).wait_send()
        mixed_send(step).wait_send()
        att_send(step).wait_send()
        out_arrived(0, mixed_in.at[:, columns(partner(step))], step)
        out_arrived(1, att_in.at[:, columns(partner(step))], step)
        return carry

    lax.fori_loop(1, shards, finish, 0)


def by_heads(gate_input, value_input, filter_taps, skip_gain, queries, keys):
    shards = lax.axis_size("ctx")
    rows, channels = value_input.shape
    width = channels // shards
    length = shards * rows
    streams = 5
    in_place = pl.BlockSpec(memory_space=pl.ANY)
    landing = pltpu.VMEM((rows, channels), jnp.bfloat16)
    shape = jax.ShapeDtypeStruct((rows, channels), jnp.bfloat16)
    forward_hi, forward_lo, inverse_hi, inverse_lo = block_transforms(rows)
    results = pl.pallas_call(
        functools.partial(fused_kernel, shards),
        out_shape=(landing, landing),
        in_specs=[in_place] * 10,
        out_specs=(in_place, in_place),
        scratch_shapes=[
            pltpu.VMEM((rows, channels), jnp.float32),
            pltpu.VMEM((rows, channels), jnp.bfloat16),
            pltpu.VMEM((length, width), jnp.bfloat16),
            pltpu.VMEM((length, width), jnp.bfloat16),
            pltpu.VMEM((length, width), jnp.bfloat16),
            pltpu.VMEM((length, width), jnp.bfloat16),
            pltpu.VMEM((length, width), jnp.bfloat16),
            pltpu.VMEM((shards, 2 * rows, width), jnp.float32),
            pltpu.VMEM((shards, 2 * rows, width), jnp.float32),
            pltpu.VMEM((shards, 2 * rows, width), jnp.float32),
            pltpu.VMEM((length, width), jnp.bfloat16),
            pltpu.VMEM((length, width), jnp.bfloat16),
            pltpu.VMEM((rows, length), jnp.float32),
            pltpu.VMEM((rows, length), jnp.bfloat16),
            pltpu.VMEM((rows, HEAD_DIM), jnp.float32),
            pltpu.VMEM((2 * rows, 2 * rows), jnp.bfloat16),
            pltpu.VMEM((2 * rows, 2 * rows), jnp.bfloat16),
            pltpu.VMEM((rows, 2 * rows), jnp.bfloat16),
            pltpu.VMEM((rows, 2 * rows), jnp.bfloat16),
            pltpu.VMEM((1, channels), jnp.float32),
            pltpu.SemaphoreType.DMA((streams,)),
            pltpu.SemaphoreType.DMA((streams, shards)),
            pltpu.SemaphoreType.DMA((streams, shards)),
            pltpu.SemaphoreType.DMA((2, shards)),
            pltpu.SemaphoreType.DMA((2, shards)),
            pltpu.SemaphoreType.DMA((2,)),
            pltpu.SemaphoreType.DMA((5,)),
        ],
        compiler_params=pltpu.CompilerParams(
            collective_id=0, has_side_effects=True, vmem_limit_bytes=56 * 1024 * 1024
        ),
        name="conv_attention",
    )(
        forward_hi, forward_lo, inverse_hi, inverse_lo, skip_gain.reshape(1, channels),
        gate_input, value_input, filter_taps, queries, keys,
    )
    return pl.pallas_call(
        hand_over,
        out_shape=(shape, shape),
        in_specs=[in_place] * 2,
        out_specs=(in_place, in_place),
        scratch_shapes=[pltpu.SemaphoreType.DMA((2, HAND_OVERS))],
        compiler_params=pltpu.CompilerParams(vmem_limit_bytes=4 * 1024 * 1024),
        name="hand_over",
    )(*results)


HAND_OVERS = 4


def hand_over(first, second, first_out, second_out, sems):
    rows = first.shape[0] // HAND_OVERS
    copies = []
    for part in range(HAND_OVERS):
        span = pl.ds(part * rows, rows)
        for number, (source, target) in enumerate(((first, first_out), (second, second_out))):
            copies.append(pltpu.make_async_copy(source.at[span, :], target.at[span, :], sems.at[number, part]))
    for copy in copies:
        copy.start()
    for copy in copies:
        copy.wait()


def per_device(gate_input, value_input, filter_taps, skip_gain, queries, keys):
    shards = lax.axis_size("ctx")
    channels = value_input.shape[1]
    whole_heads = channels % (shards * HEAD_DIM) == 0
    run = by_heads if whole_heads else by_sequence
    return run(gate_input, value_input, filter_taps, skip_gain, queries, keys)


def solution(mesh):
    placed = (
        P("ctx", "tp"),
        P("ctx", "tp"),
        P("ctx", "tp"),
        P("tp"),
        P("ctx", "tp"),
        P("ctx", "tp"),
    )
    return jax.shard_map(
        per_device,
        mesh=mesh,
        in_specs=placed,
        out_specs=(P("ctx", "tp"), P("ctx", "tp")),
        check_vma=False,
    )
```
